32 devices in a mesh: gx: 8 (over y, x, core), gy: 4 (over z).
Axes of the slice: x: 2, y: 2, z: 4, core: 2. Of those that a mesh axis runs over, the one named last changes fastest.
Arguments:
- fields: float32 [3, 8, 768, 512], P(None, None, 'gx', 'gy'), may hold values from -6 to 6
- terrain: int32 [768, 512], P('gx', 'gy'), may hold values from 0 to 2999
- parent_columns: bfloat16 [3, 60, 12288], P(None, None, ('gx', 'gy')), may hold values from -6 to 6
- record_tile: int32 [12288, 1], P(('gx', 'gy')), may hold values from 0 to 7; in each aligned block of 384 rows (0 to 383, 384 to 767, ...) at most 96 rows name the same one
- record_cells: int32 [12288, 4], P(('gx', 'gy')), may hold values from 0 to 191
- record_weights: bfloat16 [12288, 4], P(('gx', 'gy')), may hold values from 0.049804688 to 1
Outputs:
- updated_state: float32 [3, 8, 768, 512], P(None, None, 'gx', 'gy')
- nudge_coeffs: float32 [3, 8, 32, 32], replicated
The draws below stay inside these ranges and needn't reach their ends.
Inputs may be any that keep to these rules, and one draw needn't show every extreme that they name: `record_tile`: at most 96 of the 384 records of one device name the same tile index, and some device names one tile index exactly 96 times.
All inputs are finite; a program needn't handle non-finite values.
Results may differ from the reference program's by a relative error of at most 0.0003.
Values may be sent and summed in bfloat16 or wider, within the bound.
A program may use at most 64 MiB of HBM per device.

```python
import math
import jax
import jax.numpy as jnp
import numpy as np
from jax import lax

LEV = 8
PREC = 384
NVAR = 3
PL = 60
KW = 32
KT = 4
RATIO = 8
NX = 768
NY = 512
NREC = 12288
TILE_COARSE_X = 12
TILE_COARSE_Y = 16
GC = 192
NXC = 96
NYC = 64
N_GX = 8
N_GY = 4


def set_ends(drawn, own_key, smallest, high):
    dims = drawn.shape
    spot = [jax.random.randint(jax.random.fold_in(own_key, axis), (), 0, dims[axis]) for axis in range(len(dims))]
    drawn = drawn.at[tuple(spot)].set(smallest)
    longest = dims.index(max(dims))
    spot[longest] = (spot[longest] + 1) % dims[longest]
    return drawn.at[tuple(spot)].set(high)


def steps_of(stream_key, extent, cuts, least, top_value):
    gain, own = 1.0, jax.random.fold_in(stream_key, 6)
    for position, blocks in cuts:
        draws = jnp.exp(jax.random.uniform(jax.random.fold_in(own, position), (blocks,), jnp.float32, least / len(cuts), top_value / len(cuts)))
        gain = gain * jnp.repeat(draws, extent[position] // blocks).reshape([-1 if axis == position else 1 for axis in range(len(extent))])
    return gain


def assign_block(key, own, number, rows, amount, top, reach, lean):
    order = jax.random.permutation(key, amount)
    heavy_load, common = shares(amount, rows * top, reach, lean, True), shares(amount, rows * top, reach, lean, False)
    places = jnp.arange(amount)

    def named(sizes, offset_by):
        used = int((sizes > 0).sum())
        fixed = max(1, used // 4)
        shifted = fixed + (places - fixed + offset_by * (used - fixed)) % max(1, amount - fixed)
        return jnp.zeros((amount,), jnp.int32).at[order[jnp.where(places < fixed, places, shifted)]].set(jnp.asarray(sizes, jnp.int32))

    sizes = jnp.where(number % 4 == 0, named(heavy_load, number // 4), named(common, number - number // 4 - 1))
    mixed = jax.random.permutation(jax.random.fold_in(own, 3), amount)
    source_of, sink = mixed[0:amount // 2 * 2:2], mixed[1:amount // 2 * 2:2]
    slack = jnp.minimum(sizes[source_of] - 1, reach - sizes[sink]) // 2
    slack = jnp.where((source_of == order[0]) | (sink == order[0]) | (sizes[sink] == 0), 0, jnp.maximum(slack, 0))
    shifted = jax.random.randint(jax.random.fold_in(own, 4), (amount // 2,), 0, 1 << 20) % (slack + 1)
    sizes = sizes.at[source_of].add(-shifted).at[sink].add(shifted)
    items = jnp.searchsorted(jnp.cumsum(sizes), jnp.arange(rows * top), side="right").astype(jnp.int32)
    grid = items.reshape(top, rows).T
    grid = grid[jax.random.permutation(jax.random.fold_in(own, 1), rows)]
    offset_by = jax.random.randint(jax.random.fold_in(own, 2), (rows, 1), 0, top)
    return jnp.take_along_axis(grid, (jnp.arange(top)[None, :] + offset_by) % top, axis=1)


def shares(number_of, total, limit, lean, full):
    weights = [(1 << 20) // math.isqrt(rank ** lean) + 1 for rank in range(1, number_of + 1)]
    largest = limit if full else min(limit, max(-(-total // number_of), total * weights[0] // sum(weights)))
    least = 1 if total - largest >= number_of - 1 else 0
    counts, rest = [largest] + [least] * (number_of - 1), total - largest - least * (number_of - 1)
    while rest > 0:
        candidates = [i for i in range(1, number_of) if counts[i] < largest] or [i for i in range(1, number_of) if counts[i] < limit]
        pool, left = sum([weights[i] for i in candidates]), rest
        for i in candidates:
            extra = min(limit - counts[i], max(1, left * weights[i] // pool), rest)
            counts[i] = counts[i] + extra
            rest = rest - extra
    return np.array(counts)


def centred(own_key, dims, scale, bound, shards=(), held_as=jnp.bfloat16):
    level = steps_of(own_key, dims, shards, -0.22, 0.18) if shards else 1.0
    drawn = jax.random.normal(own_key, dims, jnp.float32) * scale * level
    return jnp.minimum(jnp.maximum(drawn, -bound), bound).astype(held_as)


def setup_inputs(seed: int = 0) -> dict:
    keys = jax.random.split(jax.random.key(seed), 7)
    fields = centred(keys[0], (NVAR, LEV, NX, NY), 1.0, 6.0, ((2, 8), (3, 4)), jnp.float32)
    terrain = set_ends(jax.random.randint(keys[1], (NX, NY), 0, 3000), jax.random.fold_in(keys[1], 1), 0, 2999).astype(jnp.int32)
    parent_columns = centred(keys[2], (NVAR, PL, NREC), 1.0, 6.0, ((2, 32),))
    record_tile_keys = jax.random.split(jax.random.fold_in(keys[3], 1), NREC // PREC)
    record_tile_turns = jax.random.permutation(jax.random.fold_in(keys[3], 3), NREC // PREC)
    record_tile = jax.vmap(lambda own, number: assign_block(jax.random.fold_in(keys[3], 2), own, number, PREC, N_GX, 1, 2 * PREC // N_GX, 2))(record_tile_keys, record_tile_turns).reshape((NREC, 1))
    record_cells = set_ends(jax.random.randint(keys[4], (NREC, KT), 0, GC), jax.random.fold_in(keys[4], 1), 0, GC - 1).astype(jnp.int32)
    record_weights = jnp.clip(jnp.exp(math.log(1.0) - 2.9996462 * jax.random.uniform(keys[5], (NREC, KT), jnp.float32) ** steps_of(keys[5], (NREC, KT), ((0, 32),), -0.2, 0.2)), 0.049804688, 1.0).astype(jnp.bfloat16)
    return dict(fields=fields, terrain=terrain, parent_columns=parent_columns, record_tile=record_tile, record_cells=record_cells, record_weights=record_weights)


top_height = 12000.0

def octant_table():
    half_root = math.sqrt(0.5)
    cos_table = jnp.array([1.0, half_root, 0.0, -half_root, -1.0, -half_root, 0.0, half_root, 1.0], jnp.float32)
    sin_table = jnp.array([0.0, half_root, 1.0, half_root, 0.0, -half_root, -1.0, -half_root, 0.0], jnp.float32)
    return (cos_table, sin_table)

def wave_basis(positions, length, modes):
    half = modes // 2
    orders = jnp.arange(modes, dtype=jnp.int32)
    wave_number = jnp.where(orders < half, orders, orders - half + 1)
    phase_index = (wave_number[:, None] * positions[None, :] % length).astype(jnp.int32)
    octant = ((8 * phase_index + length // 2) // length).astype(jnp.int32)
    remainder = (8 * phase_index - octant * length).astype(jnp.int32)
    small_angle = 2.0 * math.pi / (8 * length) * remainder.astype(jnp.float32)
    cos_table, sin_table = octant_table()
    octant_hot = (octant[:, :, None] == jnp.arange(9, dtype=jnp.int32)[None, None, :]).astype(jnp.float32)
    cos_octant = lax.optimization_barrier(jnp.sum(octant_hot * cos_table, axis=2))
    sin_octant = lax.optimization_barrier(jnp.sum(octant_hot * sin_table, axis=2))
    cos_small = jnp.cos(small_angle)
    sin_small = jnp.sin(small_angle)
    cos_value = cos_octant * cos_small - sin_octant * sin_small
    sin_value = sin_octant * cos_small + cos_octant * sin_small
    wave_rows = jnp.where((orders < half)[:, None], cos_value, sin_value) * math.sqrt(2.0)
    return jnp.where((orders == 0)[:, None], jnp.ones_like(wave_rows), wave_rows)

def level_weights(heights, levels, parent_levels):
    spacing = (top_height - heights) / levels
    nest_height = heights[None, :] + (jnp.arange(levels, dtype=jnp.float32)[:, None] + 0.5) * spacing[None, :]
    parent_height = (jnp.arange(parent_levels, dtype=jnp.float32) + 0.5) * (top_height / parent_levels)
    hat_weights = jnp.maximum(0.0, 1.0 - jnp.abs(nest_height[:, None, :] - parent_height[None, :, None]) / spacing[None, None, :])
    return hat_weights / lax.optimization_barrier(jnp.sum(hat_weights, axis=1, keepdims=True))

def project(values, basis_x, basis_y):
    along_x = jnp.einsum('mx,vkxy->vkmy', basis_x, values, precision=lax.Precision.HIGHEST)
    return jnp.einsum('vkmy,ny->vkmn', along_x, basis_y, precision=lax.Precision.HIGHEST)

def expand(coeffs, basis_x, basis_y):
    along_y = jnp.einsum('vkmn,ny->vkmy', coeffs, basis_y, precision=lax.Precision.HIGHEST)
    return jnp.einsum('mx,vkmy->vkxy', basis_x, along_y, precision=lax.Precision.HIGHEST)

def advance(padded, values, wind_x, wind_y, inv_metric, low_modes):
    east_side = padded[:, :, 2:, 1:-1]
    west_side = padded[:, :, :-2, 1:-1]
    north_side = padded[:, :, 1:-1, 2:]
    south_side = padded[:, :, 1:-1, :-2]
    transport = 0.5 * (wind_x * (east_side - west_side) + wind_y * (north_side - south_side))
    diffusion = east_side + west_side + north_side + south_side - 4.0 * values
    level_above = jnp.concatenate([values[:, 1:], values[:, -1:]], axis=1)
    level_below = jnp.concatenate([values[:, :1], values[:, :-1]], axis=1)
    mixing = (level_above - 2.0 * values + level_below) * inv_metric
    return values - 0.1 * transport + 0.1 * diffusion + 0.1 * mixing - 4.0 * low_modes

def reference(fields, terrain, parent_columns, record_tile, record_cells, record_weights):
    record_ids = jnp.arange(NREC, dtype=jnp.int32)
    row_y = record_ids // PREC % N_GY
    target_position = record_tile[:, 0]
    columns = parent_columns.astype(jnp.float32)
    coarse = jnp.zeros((NVAR, PL, NXC * NYC), jnp.float32)
    for entry in range(KT):
        coarse_cell_index = record_cells[:, entry]
        first_coarse_cell = target_position * TILE_COARSE_X + coarse_cell_index // TILE_COARSE_Y
        coarse_b = row_y * TILE_COARSE_Y + coarse_cell_index % TILE_COARSE_Y
        flattened_index = (first_coarse_cell * NYC + coarse_b).astype(jnp.int32)
        weight_row = record_weights[:, entry].astype(jnp.float32)
        coarse = coarse.at[:, :, flattened_index].add(columns * weight_row[None, None, :])
    heights = terrain[::RATIO, ::RATIO].reshape(-1).astype(jnp.float32)
    vertical = level_weights(heights, LEV, PL)
    target = jnp.einsum('kpg,vpg->vkg', vertical, coarse, precision=lax.Precision.HIGHEST)
    target = target.reshape(NVAR, LEV, NXC, NYC)
    basis_x = wave_basis(jnp.arange(NX, dtype=jnp.int32), NX, KW)
    basis_y = wave_basis(jnp.arange(NY, dtype=jnp.int32), NY, KW)
    scale = 1.0 / math.sqrt(NX * NY)
    nest_part = project(fields, basis_x, basis_y) * scale
    target_part = project(target, basis_x[:, ::RATIO], basis_y[:, ::RATIO]) * (RATIO * RATIO * scale)
    nudge_coeffs = nest_part - target_part
    inv_metric = jnp.square(top_height / (top_height - terrain.astype(jnp.float32)))
    results = []
    for variable in range(NVAR):
        low_modes = expand(nudge_coeffs[variable:variable + 1], basis_x, basis_y) * scale
        single = fields[variable:variable + 1]
        padded = jnp.pad(single, ((0, 0), (0, 0), (1, 1), (1, 1)))
        results.append(advance(padded, single, fields[0:1], fields[1:2], inv_metric, low_modes))
    updated_state = jnp.concatenate(results, axis=0)
    return (updated_state, nudge_coeffs)
```

```python
import functools
import math

import jax
import jax.numpy as jnp
import ml_dtypes
import numpy as np
from jax import lax
from jax.experimental import pallas as pl
from jax.experimental.pallas import tpu as pltpu
from jax.sharding import PartitionSpec as P

KW = 32
RATIO = 8
TOP = 12000.0
MESH = pl.DeviceIdType.MESH
F32 = jnp.float32
BF16 = jnp.bfloat16
NT = (((1,), (1,)), ((), ()))


def wave_rows(length):
    half = KW // 2
    x = np.arange(length, dtype=np.int64)
    rows = [np.ones(length)]
    for m in range(1, KW):
        if m < half:
            rows.append(math.sqrt(2.0) * np.cos(2.0 * math.pi * ((m * x) % length) / length))
        else:
            rows.append(
                math.sqrt(2.0) * np.sin(2.0 * math.pi * (((m - half + 1) * x) % length) / length)
            )
    return np.stack(rows)


def parts(values):
    values = values.astype(np.float32)
    high = values.astype(ml_dtypes.bfloat16)
    low = (values - high.astype(np.float32)).astype(ml_dtypes.bfloat16)
    return high, low


@functools.lru_cache(maxsize=None)
def tables(n_x, n_y, cells_x, cells_y, fields_count):
    total_x, total_y = n_x * cells_x, n_y * cells_y
    scale = 1.0 / math.sqrt(total_x * total_y)
    basis_x, basis_y = wave_rows(total_x), wave_rows(total_y)
    coarse_y = cells_y // RATIO
    own_x = np.transpose(basis_x.reshape(KW, n_x, cells_x), (1, 0, 2))
    high, low = parts(own_x * scale)
    project_x = np.concatenate(
        [np.concatenate([high, high], 2), np.concatenate([low, np.zeros_like(low)], 2)], 1
    )
    high, low = parts(np.transpose(own_x, (0, 2, 1)) * (4.0 * scale))
    expand_x = np.concatenate([high, low, high], 2)
    at_coarse = basis_x[:, ::RATIO] * (RATIO * RATIO * scale)
    coarse_x = np.kron(np.eye(4), at_coarse)
    coarse_x = np.stack(parts(coarse_x))
    own_y = np.transpose(basis_y.reshape(KW, n_y, cells_y), (1, 0, 2))
    along_y = np.stack(parts(own_y), 1)
    at_rows = np.transpose(basis_y[:, ::RATIO]).reshape(n_y, coarse_y, KW)
    coarse_y_table = np.stack(parts(np.tile(at_rows, (1, 1, fields_count))), 1).astype(np.float32)
    return project_x, expand_x, coarse_x, along_y, coarse_y_table


def split(values):
    high = values.astype(BF16)
    return high, (values - high.astype(F32)).astype(BF16)


def dot(a, b):
    return jnp.dot(a, b, preferred_element_type=F32)


def dot_nt(a, b):
    return lax.dot_general(a, b, NT, preferred_element_type=F32)


def body(
    sizes,
    fields_hbm, terrain, columns, tile, cells, weights,
    project_x_hbm, expand_x_hbm, coarse_x, along_y_hbm, coarse_y_hbm,
    state, coeffs,
    padded, column_rows, coarse, target, heights, heights_got, edge_rows, edge_rows_got,
    edge_columns, edge_columns_got, partial, partial_got, plane, total,
    project_x, expand_x, along_y, coarse_y_table, block_y, y_terms,
    load_sem, send_h, recv_h, send_e, recv_e, send_r, recv_r, send_p, recv_p, send_t, recv_t,
):
    n_x, n_y, variables, levels, parent_levels = sizes
    count = variables * levels
    cells_x, cells_y = terrain.shape
    tile_x, tile_y = cells_x // RATIO, cells_y // RATIO
    row_x = n_x * tile_x
    width = row_x * tile_y
    groups = tile_y // 4
    span = 4 * row_x
    records = tile.shape[1]
    top = 8
    me_x, me_y = lax.axis_index("gx"), lax.axis_index("gy")

    loads = [
        pltpu.make_async_copy(fields_hbm, padded.at[:, pl.ds(top, cells_x), :], load_sem.at[0]),
        pltpu.make_async_copy(project_x_hbm.at[me_x], project_x, load_sem.at[1]),
        pltpu.make_async_copy(expand_x_hbm.at[me_x], expand_x, load_sem.at[2]),
        pltpu.make_async_copy(along_y_hbm.at[me_y], along_y, load_sem.at[3]),
        pltpu.make_async_copy(coarse_y_hbm.at[me_y], coarse_y_table, load_sem.at[4]),
    ]
    for load in loads:
        load.start()

    edge_rows_got[...] = jnp.zeros_like(edge_rows_got)
    edge_columns_got[...] = jnp.zeros_like(edge_columns_got)
    barrier = pltpu.get_barrier_semaphore()
    for d in range(1, n_x):
        pl.semaphore_signal(
            barrier, inc=1, device_id=(lax.rem(me_x + d, n_x), me_y), device_id_type=MESH
        )
    for d in range(1, n_y):
        pl.semaphore_signal(
            barrier, inc=1, device_id=(me_x, lax.rem(me_y + d, n_y)), device_id_type=MESH
        )

    ground = terrain[pl.ds(0, tile_x, RATIO), :]
    low_bits = ground & 255
    ground = jnp.concatenate(
        [(ground - low_bits).astype(F32), low_bits.astype(F32)], axis=0
    ).astype(BF16)
    for g in range(groups):
        lane = lax.broadcasted_iota(jnp.int32, (cells_y, span), 1)
        row = lax.broadcasted_iota(jnp.int32, (cells_y, span), 0)
        pick = jnp.where(row == RATIO * (4 * g + lane // row_x), 1.0, 0.0).astype(BF16)
        both = dot(ground, pick)
        here = both[:tile_x] + both[tile_x:]
        lane = lax.broadcasted_iota(jnp.int32, (tile_x, span), 1)
        row = lax.broadcasted_iota(jnp.int32, (tile_x, span), 0)
        here = jnp.where(lane % row_x == me_x * tile_x + row, here, 0.0)
        heights[g : g + 1, :] = jnp.sum(here, axis=0, keepdims=True)

    pl.semaphore_wait(barrier, n_x + n_y - 2)
    sends_h = []
    for d in range(1, n_x):
        sends_h.append(
            pltpu.make_async_remote_copy(
                src_ref=heights,
                dst_ref=heights_got.at[d],
                send_sem=send_h.at[d],
                recv_sem=recv_h.at[d],
                device_id=(lax.rem(me_x + d, n_x), me_y),
                device_id_type=MESH,
            )
        )
        sends_h[-1].start()

    for load in loads:
        load.wait()

    edge_rows[0] = padded[:, top, :]
    edge_rows[1] = padded[:, top + cells_x - 1, :]
    lane = lax.broadcasted_iota(jnp.int32, (cells_x, cells_y), 1)
    first = jnp.zeros((cells_x, cells_y), F32)
    last = jnp.zeros((cells_x, cells_y), F32)
    for i in range(count):
        q = padded[i, top : top + cells_x, :]
        first = jnp.where(lane == i, q if i == 0 else pltpu.roll(q, i, 1), first)
        last = jnp.where(lane == i, pltpu.roll(q, i + 1, 1), last)
    edge_columns[0] = first
    edge_columns[1] = last

    def edge_copy(source, got, side, slot, device):
        return pltpu.make_async_remote_copy(
            src_ref=source.at[side],
            dst_ref=got.at[side],
            send_sem=send_e.at[slot],
            recv_sem=recv_e.at[slot],
            device_id=device,
            device_id_type=MESH,
        )

    down_x = edge_copy(edge_rows, edge_rows_got, 0, 0, (jnp.maximum(me_x - 1, 0), me_y))
    up_x = edge_copy(edge_rows, edge_rows_got, 1, 1, (jnp.minimum(me_x + 1, n_x - 1), me_y))
    down_y = edge_copy(edge_columns, edge_columns_got, 0, 2, (me_x, jnp.maximum(me_y - 1, 0)))
    up_y = edge_copy(edge_columns, edge_columns_got, 1, 3, (me_x, jnp.minimum(me_y + 1, n_y - 1)))
    has_down_x, has_up_x = me_x > 0, me_x < n_x - 1
    has_down_y, has_up_y = me_y > 0, me_y < n_y - 1
    edges = [
        (down_x, has_down_x, has_up_x),
        (up_x, has_up_x, has_down_x),
        (down_y, has_down_y, has_up_y),
        (up_y, has_up_y, has_down_y),
    ]
    for copy, out, _ in edges:
        pl.when(out)(copy.start)

    zero_block = jnp.zeros((KW, cells_y), BF16)
    for part in range(2):
        block = along_y[part]
        for q in range(4):
            block_y[part, q * KW : (q + 1) * KW, :] = jnp.concatenate(
                [block if q == j else zero_block for j in range(4)], axis=1
            )
    for g in range(count // 4):
        highs, lows = [], []
        for i in range(4 * g, 4 * g + 4):
            high, low = split(padded[i, top : top + cells_x, :])
            highs.append(high)
            lows.append(low)
        stacked = jnp.concatenate(
            [jnp.concatenate(highs, axis=1), jnp.concatenate(lows, axis=1)], axis=0
        )
        both = dot(project_x[...], stacked)
        y_terms[g * KW : (g + 1) * KW, :] = both[:KW] + both[KW:]
    high, low = split(y_terms[...])
    nest = dot_nt(high, block_y[0]) + dot_nt(low, block_y[0]) + dot_nt(high, block_y[1])

    column_rows[...] = jnp.zeros_like(column_rows)
    for v in range(variables):
        column_rows[v * 64 : v * 64 + parent_levels, :] = columns[v].astype(F32)
    packed = column_rows[...].astype(BF16)
    place = cells[...]
    place = (place % tile_y) * row_x + tile[...] * tile_x + place // tile_y
    amount = weights[...].astype(F32)
    step = 256 if width % 256 == 0 else 128

    def spread(i, carry):
        line = lax.broadcasted_iota(jnp.int32, (step, records), 0) + i * step
        matrix = jnp.zeros((step, records), F32)
        for e in range(place.shape[0]):
            matrix = matrix + jnp.where(place[e : e + 1] == line, amount[e : e + 1], 0.0)
        high, low = split(matrix)
        at = pl.ds(pl.multiple_of(i * step, step), step)
        coarse[:, at] = dot_nt(packed, high) + dot_nt(packed, low)
        return carry

    lax.fori_loop(0, width // step, spread, 0)

    for copy in sends_h:
        copy.wait()
    height = heights[...]
    for d in range(1, n_x):
        height = height + heights_got[d]
    heights[...] = height

    level = lax.broadcasted_iota(jnp.int32, (64, 128), 0)
    parent_height = jnp.where(
        level < parent_levels, (level.astype(F32) + 0.5) * (TOP / parent_levels), 1e9
    )
    chunks = span // 128
    for g in range(groups):

        def interpolate(j, carry):
            lanes = pl.ds(pl.multiple_of(j * 128, 128), 128)
            at = pl.ds(pl.multiple_of(g * span + j * 128, 128), 128)
            h = heights[g : g + 1, lanes]
            spacing = (TOP - h) / levels
            inverse = 1.0 / spacing
            base = h * inverse
            scaled = parent_height * inverse
            rows = [[] for _ in range(variables)]
            for k in range(levels):
                hat = jnp.maximum(0.0, 1.0 - jnp.abs((base + (k + 0.5)) - scaled))
                norm = 1.0 / jnp.sum(hat, axis=0, keepdims=True)
                for v in range(variables):
                    value = coarse[v * 64 : (v + 1) * 64, at]
                    rows[v].append(jnp.sum(hat * value, axis=0, keepdims=True) * norm)
            for v in range(variables):
                target[g * KW + v * levels : g * KW + (v + 1) * levels, lanes] = jnp.concatenate(
                    rows[v], axis=0
                )
            target[g * KW + count : (g + 1) * KW, lanes] = jnp.zeros((KW - count, 128), F32)
            return carry

        lax.fori_loop(0, chunks, interpolate, 0)

    high, low = split(target[...])
    along_x = dot_nt(coarse_x[0], high) + dot_nt(coarse_x[0], low) + dot_nt(coarse_x[1], high)
    along_x = jnp.concatenate([along_x[r * KW : (r + 1) * KW] for r in range(4)], axis=1)
    high, low = split(along_x)
    lane = lax.broadcasted_iota(jnp.int32, (KW, count * KW), 1)
    row = lax.broadcasted_iota(jnp.int32, (KW, count * KW), 0)
    own = lane // KW == row
    spread_y = []
    for part in range(2):
        blocks = []
        for r in range(4):
            for g in range(groups):
                values = coarse_y_table[part, 4 * g + r : 4 * g + r + 1, :]
                blocks.append(jnp.where(own, values, 0.0).astype(BF16))
        spread_y.append(jnp.concatenate(blocks, axis=0))
    wanted = dot(high, spread_y[0]) + dot(low, spread_y[0]) + dot(high, spread_y[1])

    lines = count // 4 * KW
    difference = [
        nest[g * KW : (g + 1) * KW] - wanted[:, g * 128 : (g + 1) * 128]
        for g in range(count // 4)
    ]
    difference = jnp.concatenate(difference, axis=0)
    piece = partial.shape[1]
    if n_x * piece != lines:
        difference = jnp.concatenate(
            [difference, jnp.zeros((n_x * piece - lines, 128), F32)], axis=0
        )
    for i in range(n_x):
        partial[i] = difference[i * piece : (i + 1) * piece]
    sends_r = []
    for d in range(1, n_x):
        to = lax.rem(me_x + d, n_x)
        sends_r.append(
            pltpu.make_async_remote_copy(
                src_ref=partial.at[to],
                dst_ref=partial_got.at[d],
                send_sem=send_r.at[d],
                recv_sem=recv_r.at[d],
                device_id=(to, me_y),
                device_id_type=MESH,
            )
        )
        sends_r[-1].start()

    for copy, out, arrives in edges:
        pl.when(out)(copy.wait_send)
        pl.when(arrives)(copy.wait_recv)
    padded[:, top + cells_x, :] = edge_rows_got[0]
    padded[:, top - 1, :] = edge_rows_got[1]
    metric = TOP / (TOP - terrain[...].astype(F32))
    metric = 0.1 * (metric * metric)

    def advance(k, carry):
        wind_x = 0.05 * padded[k, top : top + cells_x, :]
        wind_y = 0.05 * padded[levels + k, top : top + cells_x, :]
        above_k = jnp.minimum(k + 1, levels - 1)
        below_k = jnp.maximum(k - 1, 0)
        lane = lax.broadcasted_iota(jnp.int32, (cells_x, cells_y), 1)
        for v in range(variables):
            i = v * levels + k
            q = padded[i, top : top + cells_x, :]
            east = padded[i, top + 1 : top + 1 + cells_x, :]
            west = padded[i, top - 1 : top - 1 + cells_x, :]
            north = jnp.where(
                lane == cells_y - 1,
                pltpu.roll(edge_columns_got[0], cells_y - 1 - i, 1),
                pltpu.roll(q, cells_y - 1, 1),
            )
            south = jnp.where(
                lane == 0,
                pltpu.roll(edge_columns_got[1], lax.rem(cells_y - i, cells_y), 1),
                pltpu.roll(q, 1, 1),
            )
            above = padded[v * levels + above_k, top : top + cells_x, :]
            below = padded[v * levels + below_k, top : top + cells_x, :]
            transport = wind_x * (east - west) + wind_y * (north - south)
            diffusion = 0.1 * ((east + west) + (north + south) - 4.0 * q)
            mixing = metric * ((above + below) - 2.0 * q)
            state[i] = q - transport + diffusion + mixing
        return carry

    half_levels = levels // 2
    lax.fori_loop(0, half_levels, advance, 0)

    for copy in sends_r:
        copy.wait()
    mine = partial[me_x]
    for d in range(1, n_x):
        mine = mine + partial_got[d]
    plane[me_y] = mine
    sends_p = []
    for d in range(1, n_y):
        sends_p.append(
            pltpu.make_async_remote_copy(
                src_ref=plane.at[me_y],
                dst_ref=plane.at[me_y],
                send_sem=send_p.at[d],
                recv_sem=recv_p.at[d],
                device_id=(me_x, lax.rem(me_y + d, n_y)),
                device_id_type=MESH,
            )
        )
        sends_p[-1].start()
    lax.fori_loop(half_levels, levels, advance, 0)
    for copy in sends_p:
        copy.wait()
    mine = plane[0]
    for j in range(1, n_y):
        mine = mine + plane[j]
    total[me_x] = mine
    sends_t = []
    for d in range(1, n_x):
        sends_t.append(
            pltpu.make_async_remote_copy(
                src_ref=total.at[me_x],
                dst_ref=total.at[me_x],
                send_sem=send_t.at[d],
                recv_sem=recv_t.at[d],
                device_id=(lax.rem(me_x + d, n_x), me_y),
                device_id_type=MESH,
            )
        )
        sends_t[-1].start()
    for copy in sends_t:
        copy.wait()

    summed = jnp.concatenate([total[i] for i in range(n_x)], axis=0)[:lines]
    for i in range(count):
        g, q = i // 4, i % 4
        coeffs[i] = summed[g * KW : (g + 1) * KW, q * KW : (q + 1) * KW]

    high, low = split(summed)
    along = dot(high, block_y[0]) + dot(low, block_y[0]) + dot(high, block_y[1])
    for g in range(count // 4):
        high, low = split(along[g * KW : (g + 1) * KW])
        modes = dot(expand_x[...], jnp.concatenate([high, high, low], axis=0))
        for q in range(4):
            i = 4 * g + q
            state[i] = state[i] - modes[:, q * cells_y : (q + 1) * cells_y]


def per_device(sizes, fields, terrain, parent_columns, record_tile, record_cells, record_weights):
    n_x, n_y = sizes
    variables, levels, cells_x, cells_y = fields.shape
    parent_levels, records = parent_columns.shape[1:]
    count = variables * levels
    tile_x, tile_y = cells_x // RATIO, cells_y // RATIO
    row_x = n_x * tile_x
    width = row_x * tile_y
    groups = tile_y // 4
    lines = count // 4 * KW
    piece = -(-lines // (8 * n_x)) * 8
    project_x, expand_x, coarse_x, along_y, coarse_y_table = tables(
        n_x, n_y, cells_x, cells_y, count
    )
    vmem = pl.BlockSpec(memory_space=pltpu.VMEM)
    hbm = pl.BlockSpec(memory_space=pl.ANY)
    dma = pltpu.SemaphoreType.DMA
    state, coeffs = pl.pallas_call(
        functools.partial(body, (n_x, n_y, variables, levels, parent_levels)),
        out_shape=(
            jax.ShapeDtypeStruct((count, cells_x, cells_y), F32),
            jax.ShapeDtypeStruct((count, KW, KW), F32),
        ),
        in_specs=[hbm, vmem, vmem, vmem, vmem, vmem, hbm, hbm, vmem, hbm, hbm],
        out_specs=(vmem, vmem),
        scratch_shapes=[
            pltpu.VMEM((count, cells_x + 16, cells_y), F32),
            pltpu.VMEM((variables * 64, records), F32),
            pltpu.VMEM((variables * 64, width), F32),
            pltpu.VMEM((groups * KW, 4 * row_x), F32),
            pltpu.VMEM((groups, 4 * row_x), F32),
            pltpu.VMEM((n_x, groups, 4 * row_x), F32),
            pltpu.VMEM((2, count, cells_y), F32),
            pltpu.VMEM((2, count, cells_y), F32),
            pltpu.VMEM((2, cells_x, cells_y), F32),
            pltpu.VMEM((2, cells_x, cells_y), F32),
            pltpu.VMEM((n_x, piece, 128), F32),
            pltpu.VMEM((n_x, piece, 128), F32),
            pltpu.VMEM((n_y, piece, 128), F32),
            pltpu.VMEM((n_x, piece, 128), F32),
            pltpu.VMEM(project_x.shape[1:], BF16),
            pltpu.VMEM(expand_x.shape[1:], BF16),
            pltpu.VMEM(along_y.shape[1:], BF16),
            pltpu.VMEM(coarse_y_table.shape[1:], F32),
            pltpu.VMEM((2, 4 * KW, 4 * cells_y), BF16),
            pltpu.VMEM((lines, 4 * cells_y), F32),
            dma((5,)),
            dma((n_x,)), dma((n_x,)),
            dma((4,)), dma((4,)),
            dma((n_x,)), dma((n_x,)),
            dma((n_y,)), dma((n_y,)),
            dma((n_x,)), dma((n_x,)),
        ],
        compiler_params=pltpu.CompilerParams(
            collective_id=0, has_side_effects=True, vmem_limit_bytes=48 * 1024 * 1024
        ),
        name="nudge",
    )(
        fields.reshape(count, cells_x, cells_y), terrain, parent_columns,
        record_tile.T, record_cells.T, record_weights.T,
        jnp.asarray(project_x), jnp.asarray(expand_x), jnp.asarray(coarse_x),
        jnp.asarray(along_y), jnp.asarray(coarse_y_table),
    )
    return state.reshape(fields.shape), coeffs.reshape(variables, levels, KW, KW)


def solution(mesh):
    sizes = (mesh.shape["gx"], mesh.shape["gy"])
    return jax.shard_map(
        functools.partial(per_device, sizes),
        mesh=mesh,
        in_specs=(
            P(None, None, "gx", "gy"),
            P("gx", "gy"),
            P(None, None, ("gx", "gy")),
            P(("gx", "gy"), None),
            P(("gx", "gy"), None),
            P(("gx", "gy"), None),
        ),
        out_specs=(P(None, None, "gx", "gy"), P()),
        check_vma=False,
    )
```

```python
import functools
import math

import jax
import jax.numpy as jnp
import ml_dtypes
import numpy as np
from jax import lax
from jax.experimental import pallas as pl
from jax.experimental.pallas import tpu as pltpu
from jax.sharding import PartitionSpec as P

KW = 32
RATIO = 8
TOP = 12000.0
MESH = pl.DeviceIdType.MESH
F32 = jnp.float32
BF16 = jnp.bfloat16
NT = (((1,), (1,)), ((), ()))


def wave_rows(length):
    half = KW // 2
    x = np.arange(length, dtype=np.int64)
    rows = [np.ones(length)]
    for m in range(1, KW):
        if m < half:
            rows.append(math.sqrt(2.0) * np.cos(2.0 * math.pi * ((m * x) % length) / length))
        else:
            rows.append(
                math.sqrt(2.0) * np.sin(2.0 * math.pi * (((m - half + 1) * x) % length) / length)
            )
    return np.stack(rows)


def parts(values):
    values = values.astype(np.float32)
    high = values.astype(ml_dtypes.bfloat16)
    low = (values - high.astype(np.float32)).astype(ml_dtypes.bfloat16)
    return high, low


@functools.lru_cache(maxsize=None)
def tables(n_x, n_y, cells_x, cells_y, fields_count):
    total_x, total_y = n_x * cells_x, n_y * cells_y
    scale = 1.0 / math.sqrt(total_x * total_y)
    basis_x, basis_y = wave_rows(total_x), wave_rows(total_y)
    coarse_y = cells_y // RATIO
    own_x = np.transpose(basis_x.reshape(KW, n_x, cells_x), (1, 0, 2))
    high, low = parts(own_x * scale)
    project_x = np.concatenate(
        [np.concatenate([high, high], 2), np.concatenate([low, np.zeros_like(low)], 2)], 1
    )
    high, low = parts(np.transpose(own_x, (0, 2, 1)) * (4.0 * scale))
    expand_x = np.concatenate([high, low, high], 2)
    at_coarse = basis_x[:, ::RATIO] * (RATIO * RATIO * scale)
    coarse_x = np.kron(np.eye(4), at_coarse)
    coarse_x = np.stack(parts(coarse_x))
    own_y = np.transpose(basis_y.reshape(KW, n_y, cells_y), (1, 0, 2))
    along_y = np.stack(parts(own_y), 1)
    at_rows = np.transpose(basis_y[:, ::RATIO]).reshape(n_y, coarse_y, KW)
    coarse_y_table = np.stack(parts(np.tile(at_rows, (1, 1, fields_count))), 1).astype(np.float32)
    return project_x, expand_x, coarse_x, along_y, coarse_y_table


def split(values):
    high = values.astype(BF16)
    return high, (values - high.astype(F32)).astype(BF16)


def dot(a, b):
    return jnp.dot(a, b, preferred_element_type=F32)


def dot_nt(a, b):
    return lax.dot_general(a, b, NT, preferred_element_type=F32)


def body(
    sizes,
    fields_hbm, terrain_hbm, columns_hbm, tile_hbm, cells_hbm, weights_hbm,
    project_x_hbm, coarse_x_hbm, along_y_hbm, coarse_y_hbm,
    state_hbm, total_hbm,
    state, terrain, columns, tile, cells, weights, coarse_x,
    padded, column_rows, coarse, target, heights, heights_got, edge_rows, edge_rows_got,
    edge_columns, edge_columns_got, partial, partial_got, plane, total,
    project_x, along_y, coarse_y_table, y_terms,
    load_sem, store_sem, send_h, recv_h, send_e, recv_e, send_r, recv_r, send_p, recv_p, send_t, recv_t,
):
    n_x, n_y, variables, levels, parent_levels = sizes
    count = variables * levels
    cells_x, cells_y = terrain.shape
    tile_x, tile_y = cells_x // RATIO, cells_y // RATIO
    row_x = n_x * tile_x
    width = row_x * tile_y
    groups = tile_y // 4
    span = 4 * row_x
    records = tile.shape[1]
    top = 8
    me_x, me_y = lax.axis_index("gx"), lax.axis_index("gy")

    loads = [
        pltpu.make_async_copy(fields_hbm, padded.at[:, pl.ds(top, cells_x), :], load_sem.at[0]),
        pltpu.make_async_copy(project_x_hbm.at[me_x], project_x, load_sem.at[1]),
        pltpu.make_async_copy(along_y_hbm.at[me_y], along_y, load_sem.at[3]),
        pltpu.make_async_copy(coarse_y_hbm.at[me_y], coarse_y_table, load_sem.at[4]),
        pltpu.make_async_copy(coarse_x_hbm, coarse_x, load_sem.at[5]),
    ]
    early = [
        pltpu.make_async_copy(terrain_hbm, terrain, load_sem.at[6]),
        pltpu.make_async_copy(columns_hbm, columns, load_sem.at[7]),
        pltpu.make_async_copy(tile_hbm, tile, load_sem.at[8]),
        pltpu.make_async_copy(cells_hbm, cells, load_sem.at[9]),
        pltpu.make_async_copy(weights_hbm, weights, load_sem.at[10]),
    ]
    for load in early:
        load.start()
    for load in loads:
        load.start()

    edge_rows_got[...] = jnp.zeros_like(edge_rows_got)
    edge_columns_got[...] = jnp.zeros_like(edge_columns_got)
    barrier = pltpu.get_barrier_semaphore()
    for d in range(1, n_x):
        pl.semaphore_signal(
            barrier, inc=1, device_id=(lax.rem(me_x + d, n_x), me_y), device_id_type=MESH
        )
    for d in range(1, n_y):
        pl.semaphore_signal(
            barrier, inc=1, device_id=(me_x, lax.rem(me_y + d, n_y)), device_id_type=MESH
        )

    early[0].wait()
    ground = terrain[pl.ds(0, tile_x, RATIO), :]
    low_bits = ground & 255
    ground = jnp.concatenate(
        [(ground - low_bits).astype(F32), low_bits.astype(F32)], axis=0
    ).astype(BF16)
    for g in range(groups):
        lane = lax.broadcasted_iota(jnp.int32, (1, span), 1)
        row = lax.broadcasted_iota(jnp.int32, (cells_y, span), 0)
        pick = jnp.where(row == RATIO * (4 * g + lane // row_x), 1.0, 0.0).astype(BF16)
        both = dot(ground, pick)
        here = both[:tile_x] + both[tile_x:]
        row = lax.broadcasted_iota(jnp.int32, (tile_x, span), 0)
        here = jnp.where(lane % row_x - me_x * tile_x == row, here, 0.0)
        heights[g : g + 1, :] = jnp.sum(here, axis=0, keepdims=True)

    for load in early[1:]:
        load.wait()
    column_rows[...] = jnp.zeros_like(column_rows)
    for v in range(variables):
        column_rows[v * 64 : v * 64 + parent_levels, :] = columns[v].astype(F32)
    packed = column_rows[...].astype(BF16)
    place = cells[...]
    place = (place % tile_y) * row_x + tile[...] * tile_x + place // tile_y
    amount = weights[...].astype(F32)
    step = 256 if width % 256 == 0 else 128

    def spread(i, carry):
        line = lax.broadcasted_iota(jnp.int32, (step, records), 0) + i * step
        matrix = jnp.zeros((step, records), F32)
        for e in range(place.shape[0]):
            matrix = matrix + jnp.where(place[e : e + 1] == line, amount[e : e + 1], 0.0)
        high, low = split(matrix)
        at = pl.ds(pl.multiple_of(i * step, step), step)
        coarse[:, at] = dot_nt(packed, high) + dot_nt(packed, low)
        return carry

    lax.fori_loop(0, width // step, spread, 0)

    pl.semaphore_wait(barrier, n_x + n_y - 2)
    sends_h = []
    for d in range(1, n_x):
        sends_h.append(
            pltpu.make_async_remote_copy(
                src_ref=heights,
                dst_ref=heights_got.at[d],
                send_sem=send_h.at[d],
                recv_sem=recv_h.at[d],
                device_id=(lax.rem(me_x + d, n_x), me_y),
                device_id_type=MESH,
            )
        )
        sends_h[-1].start()

    for load in loads:
        load.wait()

    block_y = [diagonal(along_y[part]) for part in range(2)]
    for g in range(count // 4):
        highs, lows = [], []
        for i in range(4 * g, 4 * g + 4):
            high, low = split(padded[i, top : top + cells_x, :])
            highs.append(high)
            lows.append(low)
        stacked = jnp.concatenate(
            [jnp.concatenate(highs, axis=1), jnp.concatenate(lows, axis=1)], axis=0
        )
        both = dot(project_x[...], stacked)
        y_terms[g * KW : (g + 1) * KW, :] = both[:KW] + both[KW:]
    high, low = split(y_terms[...])
    nest = dot_nt(high, block_y[0]) + dot_nt(low, block_y[0]) + dot_nt(high, block_y[1])

    lane = lax.broadcasted_iota(jnp.int32, (KW, count * KW), 1)
    row = lax.broadcasted_iota(jnp.int32, (KW, count * KW), 0)
    own = lane // KW == row
    spread_y = []
    for part in range(2):
        blocks = []
        for r in range(4):
            for g in range(groups):
                values = coarse_y_table[part, 4 * g + r : 4 * g + r + 1, :]
                blocks.append(jnp.where(own, values, 0.0).astype(BF16))
        spread_y.append(jnp.concatenate(blocks, axis=0))

    for copy in sends_h:
        copy.wait()
    height = heights[...]
    for d in range(1, n_x):
        height = height + heights_got[d]
    heights[...] = height

    level = lax.broadcasted_iota(jnp.int32, (64, 128), 0)
    parent_height = jnp.where(
        level < parent_levels, (level.astype(F32) + 0.5) * (TOP / parent_levels), 1e9
    )
    chunks = span // 128
    for g in range(groups):

        def interpolate(j, carry):
            lanes = pl.ds(pl.multiple_of(j * 128, 128), 128)
            at = pl.ds(pl.multiple_of(g * span + j * 128, 128), 128)
            h = heights[g : g + 1, lanes]
            spacing = (TOP - h) / levels
            inverse = 1.0 / spacing
            base = h * inverse
            scaled = parent_height * inverse
            rows = [[] for _ in range(variables)]
            for k in range(levels):
                hat = jnp.maximum(0.0, 1.0 - jnp.abs((base + (k + 0.5)) - scaled))
                norm = 1.0 / jnp.sum(hat, axis=0, keepdims=True)
                for v in range(variables):
                    value = coarse[v * 64 : (v + 1) * 64, at]
                    rows[v].append(jnp.sum(hat * value, axis=0, keepdims=True) * norm)
            for v in range(variables):
                target[g * KW + v * levels : g * KW + (v + 1) * levels, lanes] = jnp.concatenate(
                    rows[v], axis=0
                )
            target[g * KW + count : (g + 1) * KW, lanes] = jnp.zeros((KW - count, 128), F32)
            return carry

        lax.fori_loop(0, chunks, interpolate, 0)

    high, low = split(target[...])
    along_x = dot_nt(coarse_x[0], high) + dot_nt(coarse_x[0], low) + dot_nt(coarse_x[1], high)
    along_x = jnp.concatenate([along_x[r * KW : (r + 1) * KW] for r in range(4)], axis=1)
    high, low = split(along_x)
    wanted = dot(high, spread_y[0]) + dot(low, spread_y[0]) + dot(high, spread_y[1])

    lines = count // 4 * KW
    difference = [
        nest[g * KW : (g + 1) * KW] - wanted[:, g * 128 : (g + 1) * 128]
        for g in range(count // 4)
    ]
    difference = jnp.concatenate(difference, axis=0)
    piece = partial.shape[1]
    if n_x * piece != lines:
        difference = jnp.concatenate(
            [difference, jnp.zeros((n_x * piece - lines, 128), F32)], axis=0
        )
    for i in range(n_x):
        partial[i] = difference[i * piece : (i + 1) * piece]
    sends_r = []
    for d in range(1, n_x):
        to = lax.rem(me_x + d, n_x)
        sends_r.append(
            pltpu.make_async_remote_copy(
                src_ref=partial.at[to],
                dst_ref=partial_got.at[d],
                send_sem=send_r.at[d],
                recv_sem=recv_r.at[d],
                device_id=(to, me_y),
                device_id_type=MESH,
            )
        )
        sends_r[-1].start()

    edge_rows[0] = padded[:, top, :]
    edge_rows[1] = padded[:, top + cells_x - 1, :]
    lane = lax.broadcasted_iota(jnp.int32, (cells_x, cells_y), 1)
    first = jnp.zeros((cells_x, cells_y), F32)
    last = jnp.zeros((cells_x, cells_y), F32)
    for i in range(count):
        q = padded[i, top : top + cells_x, :]
        first = jnp.where(lane == i, q if i == 0 else pltpu.roll(q, i, 1), first)
        last = jnp.where(lane == i, pltpu.roll(q, i + 1, 1), last)
    edge_columns[0] = first
    edge_columns[1] = last

    def edge_copy(source, got, side, slot, device):
        return pltpu.make_async_remote_copy(
            src_ref=source.at[side],
            dst_ref=got.at[side],
            send_sem=send_e.at[slot],
            recv_sem=recv_e.at[slot],
            device_id=device,
            device_id_type=MESH,
        )

    down_x = edge_copy(edge_rows, edge_rows_got, 0, 0, (jnp.maximum(me_x - 1, 0), me_y))
    up_x = edge_copy(edge_rows, edge_rows_got, 1, 1, (jnp.minimum(me_x + 1, n_x - 1), me_y))
    down_y = edge_copy(edge_columns, edge_columns_got, 0, 2, (me_x, jnp.maximum(me_y - 1, 0)))
    up_y = edge_copy(edge_columns, edge_columns_got, 1, 3, (me_x, jnp.minimum(me_y + 1, n_y - 1)))
    has_down_x, has_up_x = me_x > 0, me_x < n_x - 1
    has_down_y, has_up_y = me_y > 0, me_y < n_y - 1
    edges = [
        (down_x, has_down_x, has_up_x),
        (up_x, has_up_x, has_down_x),
        (down_y, has_down_y, has_up_y),
        (up_y, has_up_y, has_down_y),
    ]
    for copy, out, _ in edges:
        pl.when(out)(copy.start)

    metric = TOP / (TOP - terrain[...].astype(F32))
    metric = 0.1 * (metric * metric)

    def advance(k, carry):
        wind_x = 0.05 * padded[k, top : top + cells_x, :]
        wind_y = 0.05 * padded[levels + k, top : top + cells_x, :]
        above_k = jnp.minimum(k + 1, levels - 1)
        below_k = jnp.maximum(k - 1, 0)
        lane = lax.broadcasted_iota(jnp.int32, (cells_x, cells_y), 1)
        for v in range(variables):
            i = v * levels + k
            q = padded[i, top : top + cells_x, :]
            east = padded[i, top + 1 : top + 1 + cells_x, :]
            west = padded[i, top - 1 : top - 1 + cells_x, :]
            north = jnp.where(
                lane == cells_y - 1,
                pltpu.roll(edge_columns_got[0], cells_y - 1 - i, 1),
                pltpu.roll(q, cells_y - 1, 1),
            )
            south = jnp.where(
                lane == 0,
                pltpu.roll(edge_columns_got[1], lax.rem(cells_y - i, cells_y), 1),
                pltpu.roll(q, 1, 1),
            )
            above = padded[v * levels + above_k, top : top + cells_x, :]
            below = padded[v * levels + below_k, top : top + cells_x, :]
            transport = wind_x * (east - west) + wind_y * (north - south)
            diffusion = 0.1 * ((east + west) + (north + south) - 4.0 * q)
            mixing = metric * ((above + below) - 2.0 * q)
            state[i] = q - transport + diffusion + mixing
        return carry

    half_levels = levels // 2
    for copy in sends_r:
        copy.wait()
    mine = partial[me_x]
    for d in range(1, n_x):
        mine = mine + partial_got[d]
    plane[me_y] = mine
    sends_p = []
    for d in range(1, n_y):
        sends_p.append(
            pltpu.make_async_remote_copy(
                src_ref=plane.at[me_y],
                dst_ref=plane.at[me_y],
                send_sem=send_p.at[d],
                recv_sem=recv_p.at[d],
                device_id=(me_x, lax.rem(me_y + d, n_y)),
                device_id_type=MESH,
            )
        )
        sends_p[-1].start()
    for copy, out, arrives in edges:
        pl.when(out)(copy.wait_send)
        pl.when(arrives)(copy.wait_recv)
    padded[:, top + cells_x, :] = edge_rows_got[0]
    padded[:, top - 1, :] = edge_rows_got[1]

    lax.fori_loop(0, half_levels, advance, 0)
    stores = []
    for half in range(2):
        for v in range(variables):
            block = pl.ds(v * levels + half * half_levels, half_levels)
            stores.append(
                pltpu.make_async_copy(
                    state.at[block], state_hbm.at[block], store_sem.at[half * variables + v]
                )
            )
    for store in stores[:variables]:
        store.start()
    for copy in sends_p:
        copy.wait()
    mine = plane[0]
    for j in range(1, n_y):
        mine = mine + plane[j]
    total[me_x] = mine
    sends_t = []
    for d in range(1, n_x):
        sends_t.append(
            pltpu.make_async_remote_copy(
                src_ref=total.at[me_x],
                dst_ref=total.at[me_x],
                send_sem=send_t.at[d],
                recv_sem=recv_t.at[d],
                device_id=(lax.rem(me_x + d, n_x), me_y),
                device_id_type=MESH,
            )
        )
        sends_t[-1].start()
    lax.fori_loop(half_levels, levels, advance, 0)
    for store in stores[variables:]:
        store.start()
    for copy in sends_t:
        copy.wait()

    stores.append(pltpu.make_async_copy(total, total_hbm, store_sem.at[2 * variables]))
    stores[-1].start()
    for store in stores:
        store.wait()


def diagonal(block):
    empty = jnp.zeros_like(block)
    return jnp.concatenate(
        [
            jnp.concatenate([block if q == j else empty for j in range(4)], axis=1)
            for q in range(4)
        ],
        axis=0,
    )


def finish(
    partial_hbm, total_hbm, expand_x_hbm, along_y_hbm,
    state_hbm, coeffs_hbm,
    state, total, expand_x, along_y, coeffs, load_sem, store_sem,
):
    count, _, cells_y = state.shape
    n_x, piece = total.shape[:2]
    lines = count // 4 * KW
    loads = [
        pltpu.make_async_copy(total_hbm, total, load_sem.at[0]),
        pltpu.make_async_copy(along_y_hbm.at[lax.axis_index("gy")], along_y, load_sem.at[1]),
        pltpu.make_async_copy(expand_x_hbm.at[lax.axis_index("gx")], expand_x, load_sem.at[2]),
    ]
    for g in range(count // 4):
        block = pl.ds(4 * g, 4)
        loads.append(
            pltpu.make_async_copy(partial_hbm.at[block], state.at[block], load_sem.at[3 + g])
        )
    for load in loads:
        load.start()
    for load in loads[:3]:
        load.wait()
    summed = jnp.concatenate([total[i] for i in range(n_x)], axis=0)[:lines]
    for i in range(count):
        g, q = i // 4, i % 4
        coeffs[i] = summed[g * KW : (g + 1) * KW, q * KW : (q + 1) * KW]
    stores = [pltpu.make_async_copy(coeffs, coeffs_hbm, store_sem.at[0])]
    stores[0].start()
    high, low = split(summed)
    block = diagonal(along_y[0])
    along = dot(high, block) + dot(low, block) + dot(high, diagonal(along_y[1]))
    for g in range(count // 4):
        high, low = split(along[g * KW : (g + 1) * KW])
        modes = dot(expand_x[...], jnp.concatenate([high, high, low], axis=0))
        loads[3 + g].wait()
        for q in range(4):
            i = 4 * g + q
            state[i] = state[i] - modes[:, q * cells_y : (q + 1) * cells_y]
        block = pl.ds(4 * g, 4)
        stores.append(
            pltpu.make_async_copy(state.at[block], state_hbm.at[block], store_sem.at[g + 1])
        )
        stores[-1].start()
    for store in stores:
        store.wait()


def per_device(sizes, fields, terrain, parent_columns, record_tile, record_cells, record_weights):
    n_x, n_y = sizes
    variables, levels, cells_x, cells_y = fields.shape
    parent_levels, records = parent_columns.shape[1:]
    count = variables * levels
    tile_x, tile_y = cells_x // RATIO, cells_y // RATIO
    row_x = n_x * tile_x
    width = row_x * tile_y
    groups = tile_y // 4
    lines = count // 4 * KW
    piece = -(-lines // (8 * n_x)) * 8
    project_x, expand_x, coarse_x, along_y, coarse_y_table = tables(
        n_x, n_y, cells_x, cells_y, count
    )
    along_y = jnp.asarray(along_y)
    hbm = pl.BlockSpec(memory_space=pltpu.HBM)
    dma = pltpu.SemaphoreType.DMA
    partial_state, summed = pl.pallas_call(
        functools.partial(body, (n_x, n_y, variables, levels, parent_levels)),
        out_shape=(
            jax.ShapeDtypeStruct((count, cells_x, cells_y), F32),
            jax.ShapeDtypeStruct((n_x, piece, 128), F32),
        ),
        in_specs=[hbm] * 10,
        out_specs=(hbm, hbm),
        scratch_shapes=[
            pltpu.VMEM((count, cells_x, cells_y), F32),
            pltpu.VMEM(terrain.shape, jnp.int32),
            pltpu.VMEM(parent_columns.shape, BF16),
            pltpu.VMEM((1, records), jnp.int32),
            pltpu.VMEM((record_cells.shape[1], records), jnp.int32),
            pltpu.VMEM((record_cells.shape[1], records), BF16),
            pltpu.VMEM(coarse_x.shape, BF16),
            pltpu.VMEM((count, cells_x + 16, cells_y), F32),
            pltpu.VMEM((variables * 64, records), F32),
            pltpu.VMEM((variables * 64, width), F32),
            pltpu.VMEM((groups * KW, 4 * row_x), F32),
            pltpu.VMEM((groups, 4 * row_x), F32),
            pltpu.VMEM((n_x, groups, 4 * row_x), F32),
            pltpu.VMEM((2, count, cells_y), F32),
            pltpu.VMEM((2, count, cells_y), F32),
            pltpu.VMEM((2, cells_x, cells_y), F32),
            pltpu.VMEM((2, cells_x, cells_y), F32),
            pltpu.VMEM((n_x, piece, 128), F32),
            pltpu.VMEM((n_x, piece, 128), F32),
            pltpu.VMEM((n_y, piece, 128), F32),
            pltpu.VMEM((n_x, piece, 128), F32),
            pltpu.VMEM(project_x.shape[1:], BF16),
            pltpu.VMEM(along_y.shape[1:], BF16),
            pltpu.VMEM(coarse_y_table.shape[1:], F32),
            pltpu.VMEM((lines, 4 * cells_y), F32),
            dma((11,)), dma((2 * variables + 1,)),
            dma((n_x,)), dma((n_x,)),
            dma((4,)), dma((4,)),
            dma((n_x,)), dma((n_x,)),
            dma((n_y,)), dma((n_y,)),
            dma((n_x,)), dma((n_x,)),
        ],
        compiler_params=pltpu.CompilerParams(
            collective_id=0, has_side_effects=True, vmem_limit_bytes=60 * 1024 * 1024
        ),
        name="nudge",
    )(
        fields.reshape(count, cells_x, cells_y), terrain, parent_columns,
        record_tile.T, record_cells.T, record_weights.T,
        jnp.asarray(project_x), jnp.asarray(coarse_x), along_y, jnp.asarray(coarse_y_table),
    )
    state, coeffs = pl.pallas_call(
        finish,
        out_shape=(
            jax.ShapeDtypeStruct((count, cells_x, cells_y), F32),
            jax.ShapeDtypeStruct((count, KW, KW), F32),
        ),
        in_specs=[hbm] * 4,
        out_specs=(hbm, hbm),
        scratch_shapes=[
            pltpu.VMEM((count, cells_x, cells_y), F32),
            pltpu.VMEM((n_x, piece, 128), F32),
            pltpu.VMEM(expand_x.shape[1:], BF16),
            pltpu.VMEM(along_y.shape[1:], BF16),
            pltpu.VMEM((count, KW, KW), F32),
            dma((count // 4 + 3,)),
            dma((count // 4 + 1,)),
        ],
        compiler_params=pltpu.CompilerParams(vmem_limit_bytes=60 * 1024 * 1024),
        name="finish",
    )(partial_state, summed, jnp.asarray(expand_x), along_y)
    return state.reshape(fields.shape), coeffs.reshape(variables, levels, KW, KW)


def solution(mesh):
    sizes = (mesh.shape["gx"], mesh.shape["gy"])
    return jax.shard_map(
        functools.partial(per_device, sizes),
        mesh=mesh,
        in_specs=(
            P(None, None, "gx", "gy"),
            P("gx", "gy"),
            P(None, None, ("gx", "gy")),
            P(("gx", "gy"), None),
            P(("gx", "gy"), None),
            P(("gx", "gy"), None),
        ),
        out_specs=(P(None, None, "gx", "gy"), P()),
        check_vma=False,
    )
```

```python
import functools
import math

import jax
import jax.numpy as jnp
import ml_dtypes
import numpy as np
from jax import lax
from jax.experimental import pallas as pl
from jax.experimental.pallas import tpu as pltpu
from jax.sharding import PartitionSpec as P

KW = 32
RATIO = 8
TOP = 12000.0
MESH = pl.DeviceIdType.MESH
F32 = jnp.float32
BF16 = jnp.bfloat16


def wave_rows(length):
    half = KW // 2
    x = np.arange(length, dtype=np.int64)
    rows = [np.ones(length)]
    for m in range(1, KW):
        if m < half:
            rows.append(math.sqrt(2.0) * np.cos(2.0 * math.pi * ((m * x) % length) / length))
        else:
            rows.append(
                math.sqrt(2.0) * np.sin(2.0 * math.pi * (((m - half + 1) * x) % length) / length)
            )
    return np.stack(rows)


def parts(values):
    values = values.astype(np.float32)
    high = values.astype(ml_dtypes.bfloat16)
    low = (values - high.astype(np.float32)).astype(ml_dtypes.bfloat16)
    return high, low


@functools.lru_cache(maxsize=None)
def tables(n_x, n_y, cells_x, cells_y, fields_count):
    total_x, total_y = n_x * cells_x, n_y * cells_y
    scale = 1.0 / math.sqrt(total_x * total_y)
    basis_x, basis_y = wave_rows(total_x), wave_rows(total_y)
    coarse_y = cells_y // RATIO
    own_x = np.transpose(basis_x.reshape(KW, n_x, cells_x), (1, 0, 2))
    high, low = parts(own_x * scale)
    project_x = np.concatenate(
        [np.concatenate([high, high], 2), np.concatenate([low, np.zeros_like(low)], 2)], 1
    )
    high, low = parts(np.transpose(own_x, (0, 2, 1)) * (4.0 * scale))
    expand_x = np.concatenate([high, low, high], 2)
    at_coarse = basis_x[:, ::RATIO] * (RATIO * RATIO * scale)
    coarse_x = np.transpose(np.kron(np.eye(4), at_coarse))
    coarse_x = np.stack(parts(coarse_x))
    own_y = np.transpose(basis_y.reshape(KW, n_y, cells_y), (1, 0, 2))
    along_y = np.stack(parts(own_y), 1)
    project_y = np.stack(
        parts(np.stack([np.kron(np.eye(4), np.transpose(block)) for block in own_y])), 1
    )
    at_rows = np.transpose(basis_y[:, ::RATIO]).reshape(n_y, coarse_y, KW)
    coarse_y_table = np.stack(parts(np.tile(at_rows, (1, 1, fields_count))), 1).astype(np.float32)
    return project_x, expand_x, coarse_x, along_y, project_y, coarse_y_table


def split(values):
    high = values.astype(BF16)
    return high, (values - high.astype(F32)).astype(BF16)


def dot(a, b):
    return jnp.dot(a, b, preferred_element_type=F32)


def body(
    sizes,
    fields_hbm, terrain_hbm, columns_hbm, tile_hbm, cells_hbm, weights_hbm,
    project_x_hbm, coarse_x_hbm, project_y_hbm, coarse_y_hbm,
    state_hbm, total_hbm,
    state, terrain, columns, tile, cells, weights, coarse_x,
    padded, column_rows, coarse, target, heights, heights_got, edge_rows, edge_rows_got,
    edge_columns, edge_columns_got, partial, partial_got, plane, total,
    project_x, project_y, coarse_y_table, y_terms, ids, amounts,
    load_sem, store_sem, send_h, recv_h, send_e, recv_e, send_r, recv_r, send_p, recv_p, send_t, recv_t,
):
    n_x, n_y, variables, levels, parent_levels = sizes
    count = variables * levels
    cells_x, cells_y = terrain.shape
    tile_x, tile_y = cells_x // RATIO, cells_y // RATIO
    row_x = n_x * tile_x
    width = row_x * tile_y
    groups = tile_y // 4
    span = 4 * row_x
    records = tile.shape[1]
    top = 8
    me_x, me_y = lax.axis_index("gx"), lax.axis_index("gy")

    loads = [
        pltpu.make_async_copy(fields_hbm, padded.at[:, pl.ds(top, cells_x), :], load_sem.at[0]),
        pltpu.make_async_copy(project_x_hbm.at[me_x], project_x, load_sem.at[1]),
        pltpu.make_async_copy(project_y_hbm.at[me_y], project_y, load_sem.at[3]),
        pltpu.make_async_copy(coarse_y_hbm.at[me_y], coarse_y_table, load_sem.at[4]),
        pltpu.make_async_copy(coarse_x_hbm, coarse_x, load_sem.at[5]),
    ]
    early = [
        pltpu.make_async_copy(terrain_hbm, terrain, load_sem.at[6]),
        pltpu.make_async_copy(columns_hbm, columns, load_sem.at[7]),
        pltpu.make_async_copy(tile_hbm, tile, load_sem.at[8]),
        pltpu.make_async_copy(cells_hbm, cells, load_sem.at[9]),
        pltpu.make_async_copy(weights_hbm, weights, load_sem.at[10]),
    ]
    for load in early:
        load.start()
    for load in loads:
        load.start()

    edge_rows_got[...] = jnp.zeros_like(edge_rows_got)
    edge_columns_got[...] = jnp.zeros_like(edge_columns_got)
    barrier = pltpu.get_barrier_semaphore()
    for d in range(1, n_x):
        pl.semaphore_signal(
            barrier, inc=1, device_id=(lax.rem(me_x + d, n_x), me_y), device_id_type=MESH
        )
    for d in range(1, n_y):
        pl.semaphore_signal(
            barrier, inc=1, device_id=(me_x, lax.rem(me_y + d, n_y)), device_id_type=MESH
        )

    early[0].wait()
    ground = terrain[pl.ds(0, tile_x, RATIO), :]
    low_bits = ground & 255
    ground = jnp.concatenate(
        [(ground - low_bits).astype(F32), low_bits.astype(F32)], axis=0
    ).astype(BF16)
    for g in range(groups):
        lane = lax.broadcasted_iota(jnp.int32, (1, span), 1)
        row = lax.broadcasted_iota(jnp.int32, (cells_y, span), 0)
        pick = jnp.where(row == RATIO * (4 * g + lane // row_x), 1.0, 0.0).astype(BF16)
        both = dot(ground, pick)
        here = both[:tile_x] + both[tile_x:]
        row = lax.broadcasted_iota(jnp.int32, (tile_x, span), 0)
        here = jnp.where(lane % row_x - me_x * tile_x == row, here, 0.0)
        heights[g : g + 1, :] = jnp.sum(here, axis=0, keepdims=True)

    for load in early[1:]:
        load.wait()
    column_rows[...] = jnp.zeros_like(column_rows)
    for v in range(variables):
        column_rows[v * 64 : v * 64 + parent_levels, :] = columns[v].astype(F32)
    packed = column_rows[...].astype(BF16)
    place = cells[...]
    place = (place % tile_y) * row_x + tile[...] * tile_x + place // tile_y
    amount = weights[...].astype(F32)
    entries = place.shape[0]
    merged = []
    for e in range(entries):
        sum_e = jnp.zeros((1, records), F32)
        for f in range(entries):
            sum_e = sum_e + jnp.where(place[f : f + 1] == place[e : e + 1], amount[f : f + 1], 0.0)
        merged.append(sum_e)
    listed = jnp.concatenate(
        [place.astype(F32)] + merged + [jnp.zeros((128 - 2 * entries, records), F32)], axis=0
    )
    listed = jnp.transpose(listed)
    for e in range(entries):
        named = jnp.broadcast_to(listed[:, e : e + 1], (records, 128))
        ids[e] = named.astype(jnp.int32).astype(jnp.int16)
        named = jnp.broadcast_to(listed[:, entries + e : entries + e + 1], (records, 128))
        amounts[0, e], amounts[1, e] = split(named)
    step = 256 if width % 256 == 0 else 128
    lane = lax.broadcasted_iota(jnp.int32, (records, 128), 1).astype(jnp.int16)

    def spread(i, carry):
        highs, lows = [], []
        for part in range(step // 128):
            here = lane + (i * step + part * 128).astype(jnp.int16)
            high = jnp.zeros((records, 128), BF16)
            low = jnp.zeros((records, 128), BF16)
            for e in range(entries):
                hit = ids[e] == here
                high = jnp.where(hit, amounts[0, e], high)
                low = jnp.where(hit, amounts[1, e], low)
            highs.append(high)
            lows.append(low)
        at = pl.ds(pl.multiple_of(i * step, step), step)
        coarse[:, at] = dot(packed, jnp.concatenate(highs, axis=1)) + dot(
            packed, jnp.concatenate(lows, axis=1)
        )
        return carry

    lax.fori_loop(0, width // step, spread, 0)

    pl.semaphore_wait(barrier, n_x + n_y - 2)
    sends_h = []
    for d in range(1, n_x):
        sends_h.append(
            pltpu.make_async_remote_copy(
                src_ref=heights,
                dst_ref=heights_got.at[d],
                send_sem=send_h.at[d],
                recv_sem=recv_h.at[d],
                device_id=(lax.rem(me_x + d, n_x), me_y),
                device_id_type=MESH,
            )
        )
        sends_h[-1].start()

    for load in loads:
        load.wait()

    for g in range(count // 4):
        highs, lows = [], []
        for i in range(4 * g, 4 * g + 4):
            high, low = split(padded[i, top : top + cells_x, :])
            highs.append(high)
            lows.append(low)
        stacked = jnp.concatenate(
            [jnp.concatenate(highs, axis=1), jnp.concatenate(lows, axis=1)], axis=0
        )
        both = dot(project_x[...], stacked)
        y_terms[g * KW : (g + 1) * KW, :] = both[:KW] + both[KW:]
    high, low = split(y_terms[...])
    nest = dot(high, project_y[0]) + dot(low, project_y[0]) + dot(high, project_y[1])

    lane = lax.broadcasted_iota(jnp.int32, (KW, count * KW), 1)
    row = lax.broadcasted_iota(jnp.int32, (KW, count * KW), 0)
    own = lane // KW == row
    spread_y = []
    for part in range(2):
        blocks = []
        for r in range(4):
            for g in range(groups):
                values = coarse_y_table[part, 4 * g + r : 4 * g + r + 1, :]
                blocks.append(jnp.where(own, values, 0.0).astype(BF16))
        spread_y.append(jnp.concatenate(blocks, axis=0))

    for copy in sends_h:
        copy.wait()
    height = heights[...]
    for d in range(1, n_x):
        height = height + heights_got[d]
    heights[...] = height

    level = lax.broadcasted_iota(jnp.int32, (64, 128), 0)
    parent_height = jnp.where(
        level < parent_levels, (level.astype(F32) + 0.5) * (TOP / parent_levels), 1e9
    )
    chunks = span // 128
    for g in range(groups):

        def interpolate(j, carry):
            lanes = pl.ds(pl.multiple_of(j * 128, 128), 128)
            at = pl.ds(pl.multiple_of(g * span + j * 128, 128), 128)
            h = heights[g : g + 1, lanes]
            spacing = (TOP - h) / levels
            inverse = 1.0 / spacing
            base = h * inverse
            scaled = parent_height * inverse
            rows = [[] for _ in range(variables)]
            for k in range(levels):
                hat = jnp.maximum(0.0, 1.0 - jnp.abs((base + (k + 0.5)) - scaled))
                norm = 1.0 / jnp.sum(hat, axis=0, keepdims=True)
                for v in range(variables):
                    value = coarse[v * 64 : (v + 1) * 64, at]
                    rows[v].append(jnp.sum(hat * value, axis=0, keepdims=True) * norm)
            for v in range(variables):
                target[g * KW + v * levels : g * KW + (v + 1) * levels, lanes] = jnp.concatenate(
                    rows[v], axis=0
                )
            target[g * KW + count : (g + 1) * KW, lanes] = jnp.zeros((KW - count, 128), F32)
            return carry

        lax.fori_loop(0, chunks, interpolate, 0)

    high, low = split(target[...])
    along_x = dot(high, coarse_x[0]) + dot(low, coarse_x[0]) + dot(high, coarse_x[1])
    along_x = jnp.transpose(along_x)
    along_x = jnp.concatenate([along_x[r * KW : (r + 1) * KW] for r in range(4)], axis=1)
    high, low = split(along_x)
    wanted = dot(high, spread_y[0]) + dot(low, spread_y[0]) + dot(high, spread_y[1])

    lines = count // 4 * KW
    difference = [
        nest[g * KW : (g + 1) * KW] - wanted[:, g * 128 : (g + 1) * 128]
        for g in range(count // 4)
    ]
    difference = jnp.concatenate(difference, axis=0)
    piece = partial.shape[1]
    if n_x * piece != lines:
        difference = jnp.concatenate(
            [difference, jnp.zeros((n_x * piece - lines, 128), F32)], axis=0
        )
    for i in range(n_x):
        partial[i] = difference[i * piece : (i + 1) * piece]
    sends_r = []
    for d in range(1, n_x):
        to = lax.rem(me_x + d, n_x)
        sends_r.append(
            pltpu.make_async_remote_copy(
                src_ref=partial.at[to],
                dst_ref=partial_got.at[d],
                send_sem=send_r.at[d],
                recv_sem=recv_r.at[d],
                device_id=(to, me_y),
                device_id_type=MESH,
            )
        )
        sends_r[-1].start()

    edge_rows[0] = padded[:, top, :]
    edge_rows[1] = padded[:, top + cells_x - 1, :]
    lane = lax.broadcasted_iota(jnp.int32, (cells_x, cells_y), 1)
    first = jnp.zeros((cells_x, cells_y), F32)
    last = jnp.zeros((cells_x, cells_y), F32)
    for i in range(count):
        q = padded[i, top : top + cells_x, :]
        first = jnp.where(lane == i, q if i == 0 else pltpu.roll(q, i, 1), first)
        last = jnp.where(lane == i, pltpu.roll(q, i + 1, 1), last)
    edge_columns[0] = first
    edge_columns[1] = last

    def edge_copy(source, got, side, slot, device):
        return pltpu.make_async_remote_copy(
            src_ref=source.at[side],
            dst_ref=got.at[side],
            send_sem=send_e.at[slot],
            recv_sem=recv_e.at[slot],
            device_id=device,
            device_id_type=MESH,
        )

    down_x = edge_copy(edge_rows, edge_rows_got, 0, 0, (jnp.maximum(me_x - 1, 0), me_y))
    up_x = edge_copy(edge_rows, edge_rows_got, 1, 1, (jnp.minimum(me_x + 1, n_x - 1), me_y))
    down_y = edge_copy(edge_columns, edge_columns_got, 0, 2, (me_x, jnp.maximum(me_y - 1, 0)))
    up_y = edge_copy(edge_columns, edge_columns_got, 1, 3, (me_x, jnp.minimum(me_y + 1, n_y - 1)))
    has_down_x, has_up_x = me_x > 0, me_x < n_x - 1
    has_down_y, has_up_y = me_y > 0, me_y < n_y - 1
    edges = [
        (down_x, has_down_x, has_up_x),
        (up_x, has_up_x, has_down_x),
        (down_y, has_down_y, has_up_y),
        (up_y, has_up_y, has_down_y),
    ]
    for copy, out, _ in edges:
        pl.when(out)(copy.start)

    metric = TOP / (TOP - terrain[...].astype(F32))
    metric = 0.1 * (metric * metric)

    def advance(k, carry):
        wind_x = 0.05 * padded[k, top : top + cells_x, :]
        wind_y = 0.05 * padded[levels + k, top : top + cells_x, :]
        above_k = jnp.minimum(k + 1, levels - 1)
        below_k = jnp.maximum(k - 1, 0)
        lane = lax.broadcasted_iota(jnp.int32, (cells_x, cells_y), 1)
        for v in range(variables):
            i = v * levels + k
            q = padded[i, top : top + cells_x, :]
            east = padded[i, top + 1 : top + 1 + cells_x, :]
            west = padded[i, top - 1 : top - 1 + cells_x, :]
            north = jnp.where(
                lane == cells_y - 1,
                pltpu.roll(edge_columns_got[0], cells_y - 1 - i, 1),
                pltpu.roll(q, cells_y - 1, 1),
            )
            south = jnp.where(
                lane == 0,
                pltpu.roll(edge_columns_got[1], lax.rem(cells_y - i, cells_y), 1),
                pltpu.roll(q, 1, 1),
            )
            above = padded[v * levels + above_k, top : top + cells_x, :]
            below = padded[v * levels + below_k, top : top + cells_x, :]
            transport = wind_x * (east - west) + wind_y * (north - south)
            diffusion = 0.1 * ((east + west) + (north + south) - 4.0 * q)
            mixing = metric * ((above + below) - 2.0 * q)
            state[i] = q - transport + diffusion + mixing
        return carry

    half_levels = levels // 2
    for copy in sends_r:
        copy.wait()
    mine = partial[me_x]
    for d in range(1, n_x):
        mine = mine + partial_got[d]
    plane[me_y] = mine
    sends_p = []
    for d in range(1, n_y):
        sends_p.append(
            pltpu.make_async_remote_copy(
                src_ref=plane.at[me_y],
                dst_ref=plane.at[me_y],
                send_sem=send_p.at[d],
                recv_sem=recv_p.at[d],
                device_id=(me_x, lax.rem(me_y + d, n_y)),
                device_id_type=MESH,
            )
        )
        sends_p[-1].start()
    for copy, out, arrives in edges:
        pl.when(out)(copy.wait_send)
        pl.when(arrives)(copy.wait_recv)
    padded[:, top + cells_x, :] = edge_rows_got[0]
    padded[:, top - 1, :] = edge_rows_got[1]

    lax.fori_loop(0, half_levels, advance, 0)
    stores = []
    for half in range(2):
        for v in range(variables):
            block = pl.ds(v * levels + half * half_levels, half_levels)
            stores.append(
                pltpu.make_async_copy(
                    state.at[block], state_hbm.at[block], store_sem.at[half * variables + v]
                )
            )
    for store in stores[:variables]:
        store.start()
    for copy in sends_p:
        copy.wait()
    mine = plane[0]
    for j in range(1, n_y):
        mine = mine + plane[j]
    total[me_x] = mine
    sends_t = []
    for d in range(1, n_x):
        sends_t.append(
            pltpu.make_async_remote_copy(
                src_ref=total.at[me_x],
                dst_ref=total.at[me_x],
                send_sem=send_t.at[d],
                recv_sem=recv_t.at[d],
                device_id=(lax.rem(me_x + d, n_x), me_y),
                device_id_type=MESH,
            )
        )
        sends_t[-1].start()
    lax.fori_loop(half_levels, levels, advance, 0)
    for store in stores[variables:]:
        store.start()
    for copy in sends_t:
        copy.wait()

    stores.append(pltpu.make_async_copy(total, total_hbm, store_sem.at[2 * variables]))
    stores[-1].start()
    for store in stores:
        store.wait()


def diagonal(block):
    empty = jnp.zeros_like(block)
    return jnp.concatenate(
        [
            jnp.concatenate([block if q == j else empty for j in range(4)], axis=1)
            for q in range(4)
        ],
        axis=0,
    )


def finish(
    partial_hbm, total_hbm, expand_x_hbm, along_y_hbm,
    state_hbm, coeffs_hbm,
    state, total, expand_x, along_y, coeffs, load_sem, store_sem,
):
    count, _, cells_y = state.shape
    n_x, piece = total.shape[:2]
    lines = count // 4 * KW
    loads = [
        pltpu.make_async_copy(total_hbm, total, load_sem.at[0]),
        pltpu.make_async_copy(along_y_hbm.at[lax.axis_index("gy")], along_y, load_sem.at[1]),
        pltpu.make_async_copy(expand_x_hbm.at[lax.axis_index("gx")], expand_x, load_sem.at[2]),
    ]
    for g in range(count // 4):
        block = pl.ds(4 * g, 4)
        loads.append(
            pltpu.make_async_copy(partial_hbm.at[block], state.at[block], load_sem.at[3 + g])
        )
    for load in loads:
        load.start()
    for load in loads[:3]:
        load.wait()
    summed = jnp.concatenate([total[i] for i in range(n_x)], axis=0)[:lines]
    for i in range(count):
        g, q = i // 4, i % 4
        coeffs[i] = summed[g * KW : (g + 1) * KW, q * KW : (q + 1) * KW]
    stores = [pltpu.make_async_copy(coeffs, coeffs_hbm, store_sem.at[0])]
    stores[0].start()
    high, low = split(summed)
    block = diagonal(along_y[0])
    along = dot(high, block) + dot(low, block) + dot(high, diagonal(along_y[1]))
    for g in range(count // 4):
        high, low = split(along[g * KW : (g + 1) * KW])
        modes = dot(expand_x[...], jnp.concatenate([high, high, low], axis=0))
        loads[3 + g].wait()
        for q in range(4):
            i = 4 * g + q
            state[i] = state[i] - modes[:, q * cells_y : (q + 1) * cells_y]
        block = pl.ds(4 * g, 4)
        stores.append(
            pltpu.make_async_copy(state.at[block], state_hbm.at[block], store_sem.at[g + 1])
        )
        stores[-1].start()
    for store in stores:
        store.wait()


def per_device(sizes, fields, terrain, parent_columns, record_tile, record_cells, record_weights):
    n_x, n_y = sizes
    variables, levels, cells_x, cells_y = fields.shape
    parent_levels, records = parent_columns.shape[1:]
    count = variables * levels
    tile_x, tile_y = cells_x // RATIO, cells_y // RATIO
    row_x = n_x * tile_x
    width = row_x * tile_y
    groups = tile_y // 4
    lines = count // 4 * KW
    piece = -(-lines // (8 * n_x)) * 8
    project_x, expand_x, coarse_x, along_y, project_y, coarse_y_table = tables(
        n_x, n_y, cells_x, cells_y, count
    )
    along_y = jnp.asarray(along_y)
    hbm = pl.BlockSpec(memory_space=pltpu.HBM)
    dma = pltpu.SemaphoreType.DMA
    partial_state, summed = pl.pallas_call(
        functools.partial(body, (n_x, n_y, variables, levels, parent_levels)),
        out_shape=(
            jax.ShapeDtypeStruct((count, cells_x, cells_y), F32),
            jax.ShapeDtypeStruct((n_x, piece, 128), F32),
        ),
        in_specs=[hbm] * 10,
        out_specs=(hbm, hbm),
        scratch_shapes=[
            pltpu.VMEM((count, cells_x, cells_y), F32),
            pltpu.VMEM(terrain.shape, jnp.int32),
            pltpu.VMEM(parent_columns.shape, BF16),
            pltpu.VMEM((1, records), jnp.int32),
            pltpu.VMEM((record_cells.shape[1], records), jnp.int32),
            pltpu.VMEM((record_cells.shape[1], records), BF16),
            pltpu.VMEM(coarse_x.shape, BF16),
            pltpu.VMEM((count, cells_x + 16, cells_y), F32),
            pltpu.VMEM((variables * 64, records), F32),
            pltpu.VMEM((variables * 64, width), F32),
            pltpu.VMEM((groups * KW, 4 * row_x), F32),
            pltpu.VMEM((groups, 4 * row_x), F32),
            pltpu.VMEM((n_x, groups, 4 * row_x), F32),
            pltpu.VMEM((2, count, cells_y), F32),
            pltpu.VMEM((2, count, cells_y), F32),
            pltpu.VMEM((2, cells_x, cells_y), F32),
            pltpu.VMEM((2, cells_x, cells_y), F32),
            pltpu.VMEM((n_x, piece, 128), F32),
            pltpu.VMEM((n_x, piece, 128), F32),
            pltpu.VMEM((n_y, piece, 128), F32),
            pltpu.VMEM((n_x, piece, 128), F32),
            pltpu.VMEM(project_x.shape[1:], BF16),
            pltpu.VMEM(project_y.shape[1:], BF16),
            pltpu.VMEM(coarse_y_table.shape[1:], F32),
            pltpu.VMEM((lines, 4 * cells_y), F32),
            pltpu.VMEM((record_cells.shape[1], records, 128), jnp.int16),
            pltpu.VMEM((2, record_cells.shape[1], records, 128), BF16),
            dma((11,)), dma((2 * variables + 1,)),
            dma((n_x,)), dma((n_x,)),
            dma((4,)), dma((4,)),
            dma((n_x,)), dma((n_x,)),
            dma((n_y,)), dma((n_y,)),
            dma((n_x,)), dma((n_x,)),
        ],
        compiler_params=pltpu.CompilerParams(
            collective_id=0, has_side_effects=True, vmem_limit_bytes=60 * 1024 * 1024
        ),
        name="nudge",
    )(
        fields.reshape(count, cells_x, cells_y), terrain, parent_columns,
        record_tile.T, record_cells.T, record_weights.T,
        jnp.asarray(project_x), jnp.asarray(coarse_x), jnp.asarray(project_y), jnp.asarray(coarse_y_table),
    )
    state, coeffs = pl.pallas_call(
        finish,
        out_shape=(
            jax.ShapeDtypeStruct((count, cells_x, cells_y), F32),
            jax.ShapeDtypeStruct((count, KW, KW), F32),
        ),
        in_specs=[hbm] * 4,
        out_specs=(hbm, hbm),
        scratch_shapes=[
            pltpu.VMEM((count, cells_x, cells_y), F32),
            pltpu.VMEM((n_x, piece, 128), F32),
            pltpu.VMEM(expand_x.shape[1:], BF16),
            pltpu.VMEM(along_y.shape[1:], BF16),
            pltpu.VMEM((count, KW, KW), F32),
            dma((count // 4 + 3,)),
            dma((count // 4 + 1,)),
        ],
        compiler_params=pltpu.CompilerParams(vmem_limit_bytes=60 * 1024 * 1024),
        name="finish",
    )(partial_state, summed, jnp.asarray(expand_x), along_y)
    return state.reshape(fields.shape), coeffs.reshape(variables, levels, KW, KW)


def solution(mesh):
    sizes = (mesh.shape["gx"], mesh.shape["gy"])
    return jax.shard_map(
        functools.partial(per_device, sizes),
        mesh=mesh,
        in_specs=(
            P(None, None, "gx", "gy"),
            P("gx", "gy"),
            P(None, None, ("gx", "gy")),
            P(("gx", "gy"), None),
            P(("gx", "gy"), None),
            P(("gx", "gy"), None),
        ),
        out_specs=(P(None, None, "gx", "gy"), P()),
        check_vma=False,
    )
```

```python
import functools
import math

import jax
import jax.numpy as jnp
import ml_dtypes
import numpy as np
from jax import lax
from jax.experimental import pallas as pl
from jax.experimental.pallas import tpu as pltpu
from jax.sharding import PartitionSpec as P

KW = 32
RATIO = 8
TOP = 12000.0
MESH = pl.DeviceIdType.MESH
F32 = jnp.float32
BF16 = jnp.bfloat16
NT = (((1,), (1,)), ((), ()))


def wave_rows(length):
    half = KW // 2
    x = np.arange(length, dtype=np.int64)
    rows = [np.ones(length)]
    for m in range(1, KW):
        if m < half:
            rows.append(math.sqrt(2.0) * np.cos(2.0 * math.pi * ((m * x) % length) / length))
        else:
            rows.append(
                math.sqrt(2.0) * np.sin(2.0 * math.pi * (((m - half + 1) * x) % length) / length)
            )
    return np.stack(rows)


def parts(values):
    values = values.astype(np.float32)
    high = values.astype(ml_dtypes.bfloat16)
    low = (values - high.astype(np.float32)).astype(ml_dtypes.bfloat16)
    return high, low


@functools.lru_cache(maxsize=None)
def tables(n_x, n_y, cells_x, cells_y, fields_count):
    total_x, total_y = n_x * cells_x, n_y * cells_y
    scale = 1.0 / math.sqrt(total_x * total_y)
    basis_x, basis_y = wave_rows(total_x), wave_rows(total_y)
    coarse_y = cells_y // RATIO
    own_x = np.transpose(basis_x.reshape(KW, n_x, cells_x), (1, 0, 2))
    high, low = parts(own_x * scale)
    project_x = np.concatenate(
        [np.concatenate([high, high], 2), np.concatenate([low, np.zeros_like(low)], 2)], 1
    )
    high, low = parts(np.transpose(own_x, (0, 2, 1)) * (4.0 * scale))
    expand_x = np.concatenate([high, low, high], 2)
    at_coarse = basis_x[:, ::RATIO] * (RATIO * RATIO * scale)
    coarse_x = np.kron(np.eye(4), at_coarse)
    coarse_x = np.stack(parts(coarse_x))
    own_y = np.transpose(basis_y.reshape(KW, n_y, cells_y), (1, 0, 2))
    along_y = np.stack(parts(own_y), 1)
    at_rows = np.transpose(basis_y[:, ::RATIO]).reshape(n_y, coarse_y, KW)
    coarse_y_table = np.stack(parts(np.tile(at_rows, (1, 1, fields_count))), 1).astype(np.float32)
    return project_x, expand_x, coarse_x, along_y, coarse_y_table


def split(values):
    high = values.astype(BF16)
    return high, (values - high.astype(F32)).astype(BF16)


def dot(a, b):
    return jnp.dot(a, b, preferred_element_type=F32)


def dot_nt(a, b):
    return lax.dot_general(a, b, NT, preferred_element_type=F32)


def body(
    sizes,
    fields_hbm, terrain_hbm, columns_hbm, tile_hbm, cells_hbm, weights_hbm,
    project_x_hbm, coarse_x_hbm, along_y_hbm, coarse_y_hbm,
    state_hbm, total_hbm,
    state, terrain, columns, tile, cells, weights, coarse_x,
    padded, column_rows, coarse, target, heights, heights_got, edge_rows, edge_rows_got,
    edge_columns, edge_columns_got, partial, partial_got, plane, total,
    project_x, along_y, coarse_y_table, y_terms,
    load_sem, store_sem, send_h, recv_h, send_e, recv_e, send_r, recv_r, send_p, recv_p, send_t, recv_t,
):
    n_x, n_y, variables, levels, parent_levels = sizes
    count = variables * levels
    cells_x, cells_y = terrain.shape
    tile_x, tile_y = cells_x // RATIO, cells_y // RATIO
    row_x = n_x * tile_x
    width = row_x * tile_y
    groups = tile_y // 4
    span = 4 * row_x
    records = tile.shape[1]
    top = 8
    me_x, me_y = lax.axis_index("gx"), lax.axis_index("gy")

    loads = [
        pltpu.make_async_copy(fields_hbm, padded.at[:, pl.ds(top, cells_x), :], load_sem.at[0]),
        pltpu.make_async_copy(project_x_hbm.at[me_x], project_x, load_sem.at[1]),
        pltpu.make_async_copy(along_y_hbm.at[me_y], along_y, load_sem.at[3]),
        pltpu.make_async_copy(coarse_y_hbm.at[me_y], coarse_y_table, load_sem.at[4]),
        pltpu.make_async_copy(coarse_x_hbm, coarse_x, load_sem.at[5]),
    ]
    early = [
        pltpu.make_async_copy(terrain_hbm, terrain, load_sem.at[6]),
        pltpu.make_async_copy(columns_hbm, columns, load_sem.at[7]),
        pltpu.make_async_copy(tile_hbm, tile, load_sem.at[8]),
        pltpu.make_async_copy(cells_hbm, cells, load_sem.at[9]),
        pltpu.make_async_copy(weights_hbm, weights, load_sem.at[10]),
    ]
    for load in early:
        load.start()
    for load in loads:
        load.start()

    edge_rows_got[...] = jnp.zeros_like(edge_rows_got)
    edge_columns_got[...] = jnp.zeros_like(edge_columns_got)
    barrier = pltpu.get_barrier_semaphore()
    for d in range(1, n_x):
        pl.semaphore_signal(
            barrier, inc=1, device_id=(lax.rem(me_x + d, n_x), me_y), device_id_type=MESH
        )
    for d in range(1, n_y):
        pl.semaphore_signal(
            barrier, inc=1, device_id=(me_x, lax.rem(me_y + d, n_y)), device_id_type=MESH
        )

    early[0].wait()
    ground = terrain[pl.ds(0, tile_x, RATIO), :]
    low_bits = ground & 255
    ground = jnp.concatenate(
        [(ground - low_bits).astype(F32), low_bits.astype(F32)], axis=0
    ).astype(BF16)
    for g in range(groups):
        lane = lax.broadcasted_iota(jnp.int32, (1, span), 1)
        row = lax.broadcasted_iota(jnp.int32, (cells_y, span), 0)
        pick = jnp.where(row == RATIO * (4 * g + lane // row_x), 1.0, 0.0).astype(BF16)
        both = dot(ground, pick)
        here = both[:tile_x] + both[tile_x:]
        row = lax.broadcasted_iota(jnp.int32, (tile_x, span), 0)
        here = jnp.where(lane % row_x - me_x * tile_x == row, here, 0.0)
        heights[g : g + 1, :] = jnp.sum(here, axis=0, keepdims=True)

    for load in early[1:]:
        load.wait()
    column_rows[...] = jnp.zeros_like(column_rows)
    for v in range(variables):
        column_rows[v * 64 : v * 64 + parent_levels, :] = columns[v].astype(F32)
    packed = column_rows[...].astype(BF16)
    place = cells[...]
    place = (place % tile_y) * row_x + tile[...] * tile_x + place // tile_y
    amount = weights[...].astype(F32)
    entries = place.shape[0]
    merged = []
    for e in range(entries):
        sum_e = jnp.zeros((1, records), F32)
        for f in range(entries):
            sum_e = sum_e + jnp.where(place[f : f + 1] == place[e : e + 1], amount[f : f + 1], 0.0)
        merged.append(sum_e)
    step = 256 if width % 256 == 0 else 128
    line = lax.broadcasted_iota(jnp.int32, (32, records), 0)

    def spread(i, carry):
        highs, lows = [], []
        for part in range(step // 32):
            here = place - (i * step + part * 32)
            matrix = jnp.zeros((32, records), F32)
            for e in range(entries):
                matrix = jnp.where(here[e : e + 1] == line, merged[e], matrix)
            high, low = split(matrix)
            highs.append(high)
            lows.append(low)
        at = pl.ds(pl.multiple_of(i * step, step), step)
        coarse[:, at] = dot_nt(packed, jnp.concatenate(highs, axis=0)) + dot_nt(
            packed, jnp.concatenate(lows, axis=0)
        )
        return carry

    lax.fori_loop(0, width // step, spread, 0)

    pl.semaphore_wait(barrier, n_x + n_y - 2)
    sends_h = []
    for d in range(1, n_x):
        sends_h.append(
            pltpu.make_async_remote_copy(
                src_ref=heights,
                dst_ref=heights_got.at[d],
                send_sem=send_h.at[d],
                recv_sem=recv_h.at[d],
                device_id=(lax.rem(me_x + d, n_x), me_y),
                device_id_type=MESH,
            )
        )
        sends_h[-1].start()

    for load in loads:
        load.wait()

    block_y = [diagonal(along_y[part]) for part in range(2)]
    for g in range(count // 4):
        highs, lows = [], []
        for i in range(4 * g, 4 * g + 4):
            high, low = split(padded[i, top : top + cells_x, :])
            highs.append(high)
            lows.append(low)
        stacked = jnp.concatenate(
            [jnp.concatenate(highs, axis=1), jnp.concatenate(lows, axis=1)], axis=0
        )
        both = dot(project_x[...], stacked)
        y_terms[g * KW : (g + 1) * KW, :] = both[:KW] + both[KW:]
    high, low = split(y_terms[...])
    nest = dot_nt(jnp.concatenate([high, low], axis=0), block_y[0])
    nest = nest[: high.shape[0]] + nest[high.shape[0] :] + dot_nt(high, block_y[1])

    lane = lax.broadcasted_iota(jnp.int32, (KW, count * KW), 1)
    row = lax.broadcasted_iota(jnp.int32, (KW, count * KW), 0)
    own = lane // KW == row
    spread_y = []
    for part in range(2):
        blocks = []
        for r in range(4):
            for g in range(groups):
                values = coarse_y_table[part, 4 * g + r : 4 * g + r + 1, :]
                blocks.append(jnp.where(own, values, 0.0).astype(BF16))
        spread_y.append(jnp.concatenate(blocks, axis=0))

    for copy in sends_h:
        copy.wait()
    height = heights[...]
    for d in range(1, n_x):
        height = height + heights_got[d]
    heights[...] = height

    level = lax.broadcasted_iota(jnp.int32, (64, 128), 0)
    parent_height = jnp.where(
        level < parent_levels, (level.astype(F32) + 0.5) * (TOP / parent_levels), 1e9
    )
    chunks = span // 128
    for g in range(groups):

        def interpolate(j, carry):
            lanes = pl.ds(pl.multiple_of(j * 128, 128), 128)
            at = pl.ds(pl.multiple_of(g * span + j * 128, 128), 128)
            h = heights[g : g + 1, lanes]
            spacing = (TOP - h) / levels
            inverse = 1.0 / spacing
            base = h * inverse
            scaled = parent_height * inverse
            rows = [[] for _ in range(variables)]
            for k in range(levels):
                hat = jnp.maximum(0.0, 1.0 - jnp.abs((base + (k + 0.5)) - scaled))
                norm = 1.0 / jnp.sum(hat, axis=0, keepdims=True)
                for v in range(variables):
                    value = coarse[v * 64 : (v + 1) * 64, at]
                    rows[v].append(jnp.sum(hat * value, axis=0, keepdims=True) * norm)
            for v in range(variables):
                target[g * KW + v * levels : g * KW + (v + 1) * levels, lanes] = jnp.concatenate(
                    rows[v], axis=0
                )
            target[g * KW + count : (g + 1) * KW, lanes] = jnp.zeros((KW - count, 128), F32)
            return carry

        lax.fori_loop(0, chunks, interpolate, 0)

    high, low = split(target[...])
    along_x = dot_nt(coarse_x[0], high) + dot_nt(coarse_x[0], low) + dot_nt(coarse_x[1], high)
    along_x = jnp.concatenate([along_x[r * KW : (r + 1) * KW] for r in range(4)], axis=1)
    high, low = split(along_x)
    wanted = dot(jnp.concatenate([high, low], axis=0), spread_y[0])
    wanted = wanted[:KW] + wanted[KW:] + dot(high, spread_y[1])

    lines = count // 4 * KW
    difference = [
        nest[g * KW : (g + 1) * KW] - wanted[:, g * 128 : (g + 1) * 128]
        for g in range(count // 4)
    ]
    difference = jnp.concatenate(difference, axis=0)
    piece = partial.shape[1]
    if n_x * piece != lines:
        difference = jnp.concatenate(
            [difference, jnp.zeros((n_x * piece - lines, 128), F32)], axis=0
        )
    for i in range(n_x):
        partial[i] = difference[i * piece : (i + 1) * piece]
    sends_r = []
    for d in range(1, n_x):
        to = lax.rem(me_x + d, n_x)
        sends_r.append(
            pltpu.make_async_remote_copy(
                src_ref=partial.at[to],
                dst_ref=partial_got.at[d],
                send_sem=send_r.at[d],
                recv_sem=recv_r.at[d],
                device_id=(to, me_y),
                device_id_type=MESH,
            )
        )
        sends_r[-1].start()

    edge_rows[0] = padded[:, top, :]
    edge_rows[1] = padded[:, top + cells_x - 1, :]
    lane = lax.broadcasted_iota(jnp.int32, (cells_x, cells_y), 1)
    first = jnp.zeros((cells_x, cells_y), F32)
    last = jnp.zeros((cells_x, cells_y), F32)
    for i in range(count):
        q = padded[i, top : top + cells_x, :]
        first = jnp.where(lane == i, q if i == 0 else pltpu.roll(q, i, 1), first)
        last = jnp.where(lane == i, pltpu.roll(q, i + 1, 1), last)
    edge_columns[0] = first
    edge_columns[1] = last

    def edge_copy(source, got, side, slot, device):
        return pltpu.make_async_remote_copy(
            src_ref=source.at[side],
            dst_ref=got.at[side],
            send_sem=send_e.at[slot],
            recv_sem=recv_e.at[slot],
            device_id=device,
            device_id_type=MESH,
        )

    down_x = edge_copy(edge_rows, edge_rows_got, 0, 0, (jnp.maximum(me_x - 1, 0), me_y))
    up_x = edge_copy(edge_rows, edge_rows_got, 1, 1, (jnp.minimum(me_x + 1, n_x - 1), me_y))
    down_y = edge_copy(edge_columns, edge_columns_got, 0, 2, (me_x, jnp.maximum(me_y - 1, 0)))
    up_y = edge_copy(edge_columns, edge_columns_got, 1, 3, (me_x, jnp.minimum(me_y + 1, n_y - 1)))
    has_down_x, has_up_x = me_x > 0, me_x < n_x - 1
    has_down_y, has_up_y = me_y > 0, me_y < n_y - 1
    edges = [
        (down_x, has_down_x, has_up_x),
        (up_x, has_up_x, has_down_x),
        (down_y, has_down_y, has_up_y),
        (up_y, has_up_y, has_down_y),
    ]
    for copy, out, _ in edges:
        pl.when(out)(copy.start)

    rows = 32

    def advance(k, carry):
        above_k = jnp.minimum(k + 1, levels - 1)
        below_k = jnp.maximum(k - 1, 0)
        lane = lax.broadcasted_iota(jnp.int32, (rows, cells_y), 1)
        for r in range(0, cells_x, rows):
            here = slice(top + r, top + r + rows)
            metric = TOP / (TOP - terrain[r : r + rows].astype(F32))
            metric = 0.1 * (metric * metric)
            wind_x = 0.05 * padded[k, here, :]
            wind_y = 0.05 * padded[levels + k, here, :]
            for v in range(variables):
                i = v * levels + k
                q = padded[i, here, :]
                east = padded[i, top + r + 1 : top + r + 1 + rows, :]
                west = padded[i, top + r - 1 : top + r - 1 + rows, :]
                north = jnp.where(
                    lane == cells_y - 1,
                    pltpu.roll(edge_columns_got[0, r : r + rows], cells_y - 1 - i, 1),
                    pltpu.roll(q, cells_y - 1, 1),
                )
                south = jnp.where(
                    lane == 0,
                    pltpu.roll(edge_columns_got[1, r : r + rows], lax.rem(cells_y - i, cells_y), 1),
                    pltpu.roll(q, 1, 1),
                )
                above = padded[v * levels + above_k, here, :]
                below = padded[v * levels + below_k, here, :]
                transport = wind_x * (east - west) + wind_y * (north - south)
                diffusion = 0.1 * ((east + west) + (north + south) - 4.0 * q)
                mixing = metric * ((above + below) - 2.0 * q)
                state[i, r : r + rows] = q - transport + diffusion + mixing
        return carry

    half_levels = levels // 2
    for copy in sends_r:
        copy.wait()
    mine = partial[me_x]
    for d in range(1, n_x):
        mine = mine + partial_got[d]
    plane[me_y] = mine
    sends_p = []
    for d in range(1, n_y):
        sends_p.append(
            pltpu.make_async_remote_copy(
                src_ref=plane.at[me_y],
                dst_ref=plane.at[me_y],
                send_sem=send_p.at[d],
                recv_sem=recv_p.at[d],
                device_id=(me_x, lax.rem(me_y + d, n_y)),
                device_id_type=MESH,
            )
        )
        sends_p[-1].start()
    for copy, out, arrives in edges:
        pl.when(out)(copy.wait_send)
        pl.when(arrives)(copy.wait_recv)
    padded[:, top + cells_x, :] = edge_rows_got[0]
    padded[:, top - 1, :] = edge_rows_got[1]

    lax.fori_loop(0, half_levels, advance, 0)
    stores = []
    for half in range(2):
        for v in range(variables):
            block = pl.ds(v * levels + half * half_levels, half_levels)
            stores.append(
                pltpu.make_async_copy(
                    state.at[block], state_hbm.at[block], store_sem.at[half * variables + v]
                )
            )
    for store in stores[:variables]:
        store.start()
    for copy in sends_p:
        copy.wait()
    mine = plane[0]
    for j in range(1, n_y):
        mine = mine + plane[j]
    total[me_x] = mine
    sends_t = []
    for d in range(1, n_x):
        sends_t.append(
            pltpu.make_async_remote_copy(
                src_ref=total.at[me_x],
                dst_ref=total.at[me_x],
                send_sem=send_t.at[d],
                recv_sem=recv_t.at[d],
                device_id=(lax.rem(me_x + d, n_x), me_y),
                device_id_type=MESH,
            )
        )
        sends_t[-1].start()
    lax.fori_loop(half_levels, levels, advance, 0)
    for store in stores[variables:]:
        store.start()
    for copy in sends_t:
        copy.wait()

    stores.append(pltpu.make_async_copy(total, total_hbm, store_sem.at[2 * variables]))
    stores[-1].start()
    for store in stores:
        store.wait()


def diagonal(block):
    empty = jnp.zeros_like(block)
    return jnp.concatenate(
        [
            jnp.concatenate([block if q == j else empty for j in range(4)], axis=1)
            for q in range(4)
        ],
        axis=0,
    )


def finish(
    partial_hbm, total_hbm, expand_x_hbm, along_y_hbm,
    state_hbm, coeffs_hbm,
    state, total, expand_x, along_y, coeffs, load_sem, store_sem,
):
    count, _, cells_y = state.shape
    n_x, piece = total.shape[:2]
    lines = count // 4 * KW
    loads = [
        pltpu.make_async_copy(total_hbm, total, load_sem.at[0]),
        pltpu.make_async_copy(along_y_hbm.at[lax.axis_index("gy")], along_y, load_sem.at[1]),
        pltpu.make_async_copy(expand_x_hbm.at[lax.axis_index("gx")], expand_x, load_sem.at[2]),
    ]
    for g in range(count // 4):
        block = pl.ds(4 * g, 4)
        loads.append(
            pltpu.make_async_copy(partial_hbm.at[block], state.at[block], load_sem.at[3 + g])
        )
    for load in loads:
        load.start()
    for load in loads[:3]:
        load.wait()
    summed = jnp.concatenate([total[i] for i in range(n_x)], axis=0)[:lines]
    for i in range(count):
        g, q = i // 4, i % 4
        coeffs[i] = summed[g * KW : (g + 1) * KW, q * KW : (q + 1) * KW]
    stores = [pltpu.make_async_copy(coeffs, coeffs_hbm, store_sem.at[0])]
    stores[0].start()
    high, low = split(summed)
    block = diagonal(along_y[0])
    along = dot(jnp.concatenate([high, low], axis=0), block)
    along = along[:lines] + along[lines:] + dot(high, diagonal(along_y[1]))
    for g in range(count // 4):
        high, low = split(along[g * KW : (g + 1) * KW])
        modes = dot(expand_x[...], jnp.concatenate([high, high, low], axis=0))
        loads[3 + g].wait()
        for q in range(4):
            i = 4 * g + q
            state[i] = state[i] - modes[:, q * cells_y : (q + 1) * cells_y]
        block = pl.ds(4 * g, 4)
        stores.append(
            pltpu.make_async_copy(state.at[block], state_hbm.at[block], store_sem.at[g + 1])
        )
        stores[-1].start()
    for store in stores:
        store.wait()


def per_device(sizes, fields, terrain, parent_columns, record_tile, record_cells, record_weights):
    n_x, n_y = sizes
    variables, levels, cells_x, cells_y = fields.shape
    parent_levels, records = parent_columns.shape[1:]
    count = variables * levels
    tile_x, tile_y = cells_x // RATIO, cells_y // RATIO
    row_x = n_x * tile_x
    width = row_x * tile_y
    groups = tile_y // 4
    lines = count // 4 * KW
    piece = -(-lines // (8 * n_x)) * 8
    project_x, expand_x, coarse_x, along_y, coarse_y_table = tables(
        n_x, n_y, cells_x, cells_y, count
    )
    along_y = jnp.asarray(along_y)
    hbm = pl.BlockSpec(memory_space=pltpu.HBM)
    dma = pltpu.SemaphoreType.DMA
    partial_state, summed = pl.pallas_call(
        functools.partial(body, (n_x, n_y, variables, levels, parent_levels)),
        out_shape=(
            jax.ShapeDtypeStruct((count, cells_x, cells_y), F32),
            jax.ShapeDtypeStruct((n_x, piece, 128), F32),
        ),
        in_specs=[hbm] * 10,
        out_specs=(hbm, hbm),
        scratch_shapes=[
            pltpu.VMEM((count, cells_x, cells_y), F32),
            pltpu.VMEM(terrain.shape, jnp.int32),
            pltpu.VMEM(parent_columns.shape, BF16),
            pltpu.VMEM((1, records), jnp.int32),
            pltpu.VMEM((record_cells.shape[1], records), jnp.int32),
            pltpu.VMEM((record_cells.shape[1], records), BF16),
            pltpu.VMEM(coarse_x.shape, BF16),
            pltpu.VMEM((count, cells_x + 16, cells_y), F32),
            pltpu.VMEM((variables * 64, records), F32),
            pltpu.VMEM((variables * 64, width), F32),
            pltpu.VMEM((groups * KW, 4 * row_x), F32),
            pltpu.VMEM((groups, 4 * row_x), F32),
            pltpu.VMEM((n_x, groups, 4 * row_x), F32),
            pltpu.VMEM((2, count, cells_y), F32),
            pltpu.VMEM((2, count, cells_y), F32),
            pltpu.VMEM((2, cells_x, cells_y), F32),
            pltpu.VMEM((2, cells_x, cells_y), F32),
            pltpu.VMEM((n_x, piece, 128), F32),
            pltpu.VMEM((n_x, piece, 128), F32),
            pltpu.VMEM((n_y, piece, 128), F32),
            pltpu.VMEM((n_x, piece, 128), F32),
            pltpu.VMEM(project_x.shape[1:], BF16),
            pltpu.VMEM(along_y.shape[1:], BF16),
            pltpu.VMEM(coarse_y_table.shape[1:], F32),
            pltpu.VMEM((lines, 4 * cells_y), F32),
            dma((11,)), dma((2 * variables + 1,)),
            dma((n_x,)), dma((n_x,)),
            dma((4,)), dma((4,)),
            dma((n_x,)), dma((n_x,)),
            dma((n_y,)), dma((n_y,)),
            dma((n_x,)), dma((n_x,)),
        ],
        compiler_params=pltpu.CompilerParams(
            collective_id=0, has_side_effects=True, vmem_limit_bytes=60 * 1024 * 1024
        ),
        name="nudge",
    )(
        fields.reshape(count, cells_x, cells_y), terrain, parent_columns,
        record_tile.T, record_cells.T, record_weights.T,
        jnp.asarray(project_x), jnp.asarray(coarse_x), along_y, jnp.asarray(coarse_y_table),
    )
    state, coeffs = pl.pallas_call(
        finish,
        out_shape=(
            jax.ShapeDtypeStruct((count, cells_x, cells_y), F32),
            jax.ShapeDtypeStruct((count, KW, KW), F32),
        ),
        in_specs=[hbm] * 4,
        out_specs=(hbm, hbm),
        scratch_shapes=[
            pltpu.VMEM((count, cells_x, cells_y), F32),
            pltpu.VMEM((n_x, piece, 128), F32),
            pltpu.VMEM(expand_x.shape[1:], BF16),
            pltpu.VMEM(along_y.shape[1:], BF16),
            pltpu.VMEM((count, KW, KW), F32),
            dma((count // 4 + 3,)),
            dma((count // 4 + 1,)),
        ],
        compiler_params=pltpu.CompilerParams(vmem_limit_bytes=60 * 1024 * 1024),
        name="finish",
    )(partial_state, summed, jnp.asarray(expand_x), along_y)
    return state.reshape(fields.shape), coeffs.reshape(variables, levels, KW, KW)


def solution(mesh):
    sizes = (mesh.shape["gx"], mesh.shape["gy"])
    return jax.shard_map(
        functools.partial(per_device, sizes),
        mesh=mesh,
        in_specs=(
            P(None, None, "gx", "gy"),
            P("gx", "gy"),
            P(None, None, ("gx", "gy")),
            P(("gx", "gy"), None),
            P(("gx", "gy"), None),
            P(("gx", "gy"), None),
        ),
        out_specs=(P(None, None, "gx", "gy"), P()),
        check_vma=False,
    )
```

```python
import functools
import math

import jax
import jax.numpy as jnp
import ml_dtypes
import numpy as np
from jax import lax
from jax.experimental import pallas as pl
from jax.experimental.pallas import tpu as pltpu
from jax.sharding import PartitionSpec as P

KW = 32
RATIO = 8
TOP = 12000.0
MESH = pl.DeviceIdType.MESH
F32 = jnp.float32
BF16 = jnp.bfloat16
NT = (((1,), (1,)), ((), ()))


def wave_rows(length):
    half = KW // 2
    x = np.arange(length, dtype=np.int64)
    rows = [np.ones(length)]
    for m in range(1, KW):
        if m < half:
            rows.append(math.sqrt(2.0) * np.cos(2.0 * math.pi * ((m * x) % length) / length))
        else:
            rows.append(
                math.sqrt(2.0) * np.sin(2.0 * math.pi * (((m - half + 1) * x) % length) / length)
            )
    return np.stack(rows)


def parts(values):
    values = values.astype(np.float32)
    high = values.astype(ml_dtypes.bfloat16)
    low = (values - high.astype(np.float32)).astype(ml_dtypes.bfloat16)
    return high, low


@functools.lru_cache(maxsize=None)
def tables(n_x, n_y, cells_x, cells_y, fields_count):
    total_x, total_y = n_x * cells_x, n_y * cells_y
    scale = 1.0 / math.sqrt(total_x * total_y)
    basis_x, basis_y = wave_rows(total_x), wave_rows(total_y)
    coarse_y = cells_y // RATIO
    own_x = np.transpose(basis_x.reshape(KW, n_x, cells_x), (1, 0, 2))
    high, low = parts(own_x * scale)
    project_x = np.concatenate(
        [np.concatenate([high, high], 2), np.concatenate([low, np.zeros_like(low)], 2)], 1
    )
    high, low = parts(np.transpose(own_x, (0, 2, 1)) * (4.0 * scale))
    expand_x = np.concatenate([high, low, high], 2)
    at_coarse = basis_x[:, ::RATIO] * (RATIO * RATIO * scale)
    coarse_x = np.kron(np.eye(4), at_coarse)
    coarse_x = np.stack(parts(coarse_x))
    own_y = np.transpose(basis_y.reshape(KW, n_y, cells_y), (1, 0, 2))
    along_y = np.stack(parts(own_y), 1)
    at_rows = np.transpose(basis_y[:, ::RATIO]).reshape(n_y, coarse_y, KW)
    coarse_y_table = np.stack(parts(np.tile(at_rows, (1, 1, fields_count))), 1).astype(np.float32)
    return project_x, expand_x, coarse_x, along_y, coarse_y_table


def split(values):
    high = values.astype(BF16)
    return high, (values - high.astype(F32)).astype(BF16)


def dot(a, b):
    return jnp.dot(a, b, preferred_element_type=F32)


def dot_nt(a, b):
    return lax.dot_general(a, b, NT, preferred_element_type=F32)


def body(
    sizes,
    fields_hbm, terrain_hbm, columns_hbm, tile_hbm, cells_hbm, weights_hbm,
    project_x_hbm, coarse_x_hbm, along_y_hbm, coarse_y_hbm,
    state_hbm, total_hbm,
    state, terrain, columns, tile, cells, weights, coarse_x,
    padded, column_rows, coarse, target, heights, heights_got, edge_rows, edge_rows_got,
    edge_columns, edge_columns_got, turned, partial, partial_got, plane, total,
    project_x, along_y, coarse_y_table, y_terms,
    load_sem, store_sem, send_h, recv_h, send_e, recv_e, send_r, recv_r, send_p, recv_p, send_t, recv_t,
):
    n_x, n_y, variables, levels, parent_levels = sizes
    count = variables * levels
    cells_x, cells_y = terrain.shape
    tile_x, tile_y = cells_x // RATIO, cells_y // RATIO
    row_x = n_x * tile_x
    width = row_x * tile_y
    groups = tile_y // 4
    span = 4 * row_x
    records = tile.shape[1]
    top = 8
    me_x, me_y = lax.axis_index("gx"), lax.axis_index("gy")

    loads = [
        pltpu.make_async_copy(fields_hbm, padded.at[:, pl.ds(top, cells_x), :], load_sem.at[0]),
        pltpu.make_async_copy(project_x_hbm.at[me_x], project_x, load_sem.at[1]),
        pltpu.make_async_copy(along_y_hbm.at[me_y], along_y, load_sem.at[3]),
        pltpu.make_async_copy(coarse_y_hbm.at[me_y], coarse_y_table, load_sem.at[4]),
        pltpu.make_async_copy(coarse_x_hbm, coarse_x, load_sem.at[5]),
    ]
    early = [
        pltpu.make_async_copy(terrain_hbm, terrain, load_sem.at[6]),
        pltpu.make_async_copy(columns_hbm, columns, load_sem.at[7]),
        pltpu.make_async_copy(tile_hbm, tile, load_sem.at[8]),
        pltpu.make_async_copy(cells_hbm, cells, load_sem.at[9]),
        pltpu.make_async_copy(weights_hbm, weights, load_sem.at[10]),
    ]
    for load in early:
        load.start()
    for load in loads:
        load.start()

    edge_rows_got[...] = jnp.zeros_like(edge_rows_got)
    edge_columns_got[...] = jnp.zeros_like(edge_columns_got)
    barrier = pltpu.get_barrier_semaphore()
    for d in range(1, n_x):
        pl.semaphore_signal(
            barrier, inc=1, device_id=(lax.rem(me_x + d, n_x), me_y), device_id_type=MESH
        )
    for d in range(1, n_y):
        pl.semaphore_signal(
            barrier, inc=1, device_id=(me_x, lax.rem(me_y + d, n_y)), device_id_type=MESH
        )

    early[0].wait()
    ground = terrain[pl.ds(0, tile_x, RATIO), :]
    low_bits = ground & 255
    ground = jnp.concatenate(
        [(ground - low_bits).astype(F32), low_bits.astype(F32)], axis=0
    ).astype(BF16)
    for g in range(groups):
        lane = lax.broadcasted_iota(jnp.int32, (1, span), 1)
        row = lax.broadcasted_iota(jnp.int32, (cells_y, span), 0)
        pick = jnp.where(row == RATIO * (4 * g + lane // row_x), 1.0, 0.0).astype(BF16)
        both = dot(ground, pick)
        here = both[:tile_x] + both[tile_x:]
        row = lax.broadcasted_iota(jnp.int32, (tile_x, span), 0)
        here = jnp.where(lane % row_x - me_x * tile_x == row, here, 0.0)
        heights[g : g + 1, :] = jnp.sum(here, axis=0, keepdims=True)

    pl.semaphore_wait(barrier, n_x + n_y - 2)
    sends_h = []
    for d in range(1, n_x):
        sends_h.append(
            pltpu.make_async_remote_copy(
                src_ref=heights,
                dst_ref=heights_got.at[d],
                send_sem=send_h.at[d],
                recv_sem=recv_h.at[d],
                device_id=(lax.rem(me_x + d, n_x), me_y),
                device_id_type=MESH,
            )
        )
        sends_h[-1].start()

    for load in early[1:]:
        load.wait()
    column_rows[...] = jnp.zeros_like(column_rows)
    for v in range(variables):
        column_rows[v * 64 : v * 64 + parent_levels, :] = columns[v].astype(F32)
    packed = column_rows[...].astype(BF16)
    place = cells[...]
    place = (place % tile_y) * row_x + tile[...] * tile_x + place // tile_y
    amount = weights[...].astype(F32)
    entries = place.shape[0]
    merged = []
    for e in range(entries):
        sum_e = jnp.zeros((1, records), F32)
        for f in range(entries):
            sum_e = sum_e + jnp.where(place[f : f + 1] == place[e : e + 1], amount[f : f + 1], 0.0)
        merged.append(sum_e)
    step = 256 if width % 256 == 0 else 128
    line = lax.broadcasted_iota(jnp.int32, (32, records), 0)

    def spread(i, carry):
        highs, lows = [], []
        for part in range(step // 32):
            here = place - (i * step + part * 32)
            matrix = jnp.zeros((32, records), F32)
            for e in range(entries):
                matrix = jnp.where(here[e : e + 1] == line, merged[e], matrix)
            high, low = split(matrix)
            highs.append(high)
            lows.append(low)
        at = pl.ds(pl.multiple_of(i * step, step), step)
        coarse[:, at] = dot_nt(packed, jnp.concatenate(highs, axis=0)) + dot_nt(
            packed, jnp.concatenate(lows, axis=0)
        )
        return carry

    lax.fori_loop(0, width // step, spread, 0)

    for load in loads:
        load.wait()

    block_y = [diagonal(along_y[part]) for part in range(2)]
    for g in range(count // 4):
        highs, lows = [], []
        for i in range(4 * g, 4 * g + 4):
            high, low = split(padded[i, top : top + cells_x, :])
            highs.append(high)
            lows.append(low)
        stacked = jnp.concatenate(
            [jnp.concatenate(highs, axis=1), jnp.concatenate(lows, axis=1)], axis=0
        )
        both = dot(project_x[...], stacked)
        y_terms[g * KW : (g + 1) * KW, :] = both[:KW] + both[KW:]
    high, low = split(y_terms[...])
    nest = dot_nt(jnp.concatenate([high, low], axis=0), block_y[0])
    nest = nest[: high.shape[0]] + nest[high.shape[0] :] + dot_nt(high, block_y[1])

    lane = lax.broadcasted_iota(jnp.int32, (KW, count * KW), 1)
    row = lax.broadcasted_iota(jnp.int32, (KW, count * KW), 0)
    own = lane // KW == row
    spread_y = []
    for part in range(2):
        blocks = []
        for r in range(4):
            for g in range(groups):
                values = coarse_y_table[part, 4 * g + r : 4 * g + r + 1, :]
                blocks.append(jnp.where(own, values, 0.0).astype(BF16))
        spread_y.append(jnp.concatenate(blocks, axis=0))

    for copy in sends_h:
        copy.wait()
    height = heights[...]
    for d in range(1, n_x):
        height = height + heights_got[d]
    heights[...] = height

    level = lax.broadcasted_iota(jnp.int32, (64, 128), 0)
    parent_height = jnp.where(
        level < parent_levels, (level.astype(F32) + 0.5) * (TOP / parent_levels), 1e9
    )
    chunks = span // 128
    for g in range(groups):

        def interpolate(j, carry):
            lanes = pl.ds(pl.multiple_of(j * 128, 128), 128)
            at = pl.ds(pl.multiple_of(g * span + j * 128, 128), 128)
            h = heights[g : g + 1, lanes]
            spacing = (TOP - h) / levels
            inverse = 1.0 / spacing
            base = h * inverse
            scaled = parent_height * inverse
            rows = [[] for _ in range(variables)]
            for k in range(levels):
                hat = jnp.maximum(0.0, 1.0 - jnp.abs((base + (k + 0.5)) - scaled))
                norm = 1.0 / jnp.sum(hat, axis=0, keepdims=True)
                for v in range(variables):
                    value = coarse[v * 64 : (v + 1) * 64, at]
                    rows[v].append(jnp.sum(hat * value, axis=0, keepdims=True) * norm)
            for v in range(variables):
                target[g * KW + v * levels : g * KW + (v + 1) * levels, lanes] = jnp.concatenate(
                    rows[v], axis=0
                )
            target[g * KW + count : (g + 1) * KW, lanes] = jnp.zeros((KW - count, 128), F32)
            return carry

        lax.fori_loop(0, chunks, interpolate, 0)

    high, low = split(target[...])
    along_x = dot_nt(coarse_x[0], high) + dot_nt(coarse_x[0], low) + dot_nt(coarse_x[1], high)
    along_x = jnp.concatenate([along_x[r * KW : (r + 1) * KW] for r in range(4)], axis=1)
    high, low = split(along_x)
    wanted = dot(jnp.concatenate([high, low], axis=0), spread_y[0])
    wanted = wanted[:KW] + wanted[KW:] + dot(high, spread_y[1])

    lines = count // 4 * KW
    difference = [
        nest[g * KW : (g + 1) * KW] - wanted[:, g * 128 : (g + 1) * 128]
        for g in range(count // 4)
    ]
    difference = jnp.concatenate(difference, axis=0)
    piece = partial.shape[1]
    if n_x * piece != lines:
        difference = jnp.concatenate(
            [difference, jnp.zeros((n_x * piece - lines, 128), F32)], axis=0
        )
    for i in range(n_x):
        partial[i] = difference[i * piece : (i + 1) * piece]
    sends_r = []
    for d in range(1, n_x):
        to = lax.rem(me_x + d, n_x)
        sends_r.append(
            pltpu.make_async_remote_copy(
                src_ref=partial.at[to],
                dst_ref=partial_got.at[d],
                send_sem=send_r.at[d],
                recv_sem=recv_r.at[d],
                device_id=(to, me_y),
                device_id_type=MESH,
            )
        )
        sends_r[-1].start()

    edge_rows[0] = padded[:, top, :]
    edge_rows[1] = padded[:, top + cells_x - 1, :]
    lane = lax.broadcasted_iota(jnp.int32, (cells_x, cells_y), 1)
    first = jnp.zeros((cells_x, cells_y), F32)
    last = jnp.zeros((cells_x, cells_y), F32)
    for i in range(count):
        q = padded[i, top : top + cells_x, :]
        first = jnp.where(lane == i, q if i == 0 else pltpu.roll(q, i, 1), first)
        last = jnp.where(lane == i, pltpu.roll(q, i + 1, 1), last)
    for side, columns_here in enumerate((first, last)):
        columns_here = jnp.concatenate(
            [columns_here, jnp.zeros((cells_y - cells_x, cells_y), F32)], axis=0
        )
        edge_columns[side] = jnp.transpose(columns_here)[:count]

    def edge_copy(source, got, side, slot, device):
        return pltpu.make_async_remote_copy(
            src_ref=source.at[side],
            dst_ref=got.at[side],
            send_sem=send_e.at[slot],
            recv_sem=recv_e.at[slot],
            device_id=device,
            device_id_type=MESH,
        )

    down_x = edge_copy(edge_rows, edge_rows_got, 0, 0, (jnp.maximum(me_x - 1, 0), me_y))
    up_x = edge_copy(edge_rows, edge_rows_got, 1, 1, (jnp.minimum(me_x + 1, n_x - 1), me_y))
    down_y = edge_copy(edge_columns, edge_columns_got, 0, 2, (me_x, jnp.maximum(me_y - 1, 0)))
    up_y = edge_copy(edge_columns, edge_columns_got, 1, 3, (me_x, jnp.minimum(me_y + 1, n_y - 1)))
    has_down_x, has_up_x = me_x > 0, me_x < n_x - 1
    has_down_y, has_up_y = me_y > 0, me_y < n_y - 1
    edges = [
        (down_x, has_down_x, has_up_x),
        (up_x, has_up_x, has_down_x),
        (down_y, has_down_y, has_up_y),
        (up_y, has_up_y, has_down_y),
    ]
    for copy, out, _ in edges:
        pl.when(out)(copy.start)

    rows = 32

    def advance(k, carry):
        above_k = jnp.minimum(k + 1, levels - 1)
        below_k = jnp.maximum(k - 1, 0)
        lane = lax.broadcasted_iota(jnp.int32, (rows, cells_y), 1)
        for r in range(0, cells_x, rows):
            here = slice(top + r, top + r + rows)
            metric = TOP / (TOP - terrain[r : r + rows].astype(F32))
            metric = 0.1 * (metric * metric)
            wind_x = 0.05 * padded[k, here, :]
            wind_y = 0.05 * padded[levels + k, here, :]
            for v in range(variables):
                i = v * levels + k
                q = padded[i, here, :]
                east = padded[i, top + r + 1 : top + r + 1 + rows, :]
                west = padded[i, top + r - 1 : top + r - 1 + rows, :]
                north = jnp.where(
                    lane == cells_y - 1,
                    pltpu.roll(turned[0, r : r + rows], cells_y - 1 - i, 1),
                    pltpu.roll(q, cells_y - 1, 1),
                )
                south = jnp.where(
                    lane == 0,
                    pltpu.roll(turned[1, r : r + rows], lax.rem(cells_y - i, cells_y), 1),
                    pltpu.roll(q, 1, 1),
                )
                above = padded[v * levels + above_k, here, :]
                below = padded[v * levels + below_k, here, :]
                transport = wind_x * (east - west) + wind_y * (north - south)
                diffusion = 0.1 * ((east + west) + (north + south) - 4.0 * q)
                mixing = metric * ((above + below) - 2.0 * q)
                state[i, r : r + rows] = q - transport + diffusion + mixing
        return carry

    half_levels = levels // 2
    for copy in sends_r:
        copy.wait()
    mine = partial[me_x]
    for d in range(1, n_x):
        mine = mine + partial_got[d]
    plane[me_y] = mine
    sends_p = []
    for d in range(1, n_y):
        sends_p.append(
            pltpu.make_async_remote_copy(
                src_ref=plane.at[me_y],
                dst_ref=plane.at[me_y],
                send_sem=send_p.at[d],
                recv_sem=recv_p.at[d],
                device_id=(me_x, lax.rem(me_y + d, n_y)),
                device_id_type=MESH,
            )
        )
        sends_p[-1].start()
    for copy, out, arrives in edges:
        pl.when(out)(copy.wait_send)
        pl.when(arrives)(copy.wait_recv)
    for side in range(2):
        columns_here = jnp.concatenate(
            [edge_columns_got[side], jnp.zeros((cells_y - count, cells_y), F32)], axis=0
        )
        turned[side] = jnp.transpose(columns_here)[:cells_x]
    padded[:, top + cells_x, :] = edge_rows_got[0]
    padded[:, top - 1, :] = edge_rows_got[1]

    lax.fori_loop(0, half_levels, advance, 0)
    stores = []
    for half in range(2):
        for v in range(variables):
            block = pl.ds(v * levels + half * half_levels, half_levels)
            stores.append(
                pltpu.make_async_copy(
                    state.at[block], state_hbm.at[block], store_sem.at[half * variables + v]
                )
            )
    for store in stores[:variables]:
        store.start()
    for copy in sends_p:
        copy.wait()
    mine = plane[0]
    for j in range(1, n_y):
        mine = mine + plane[j]
    total[me_x] = mine
    sends_t = []
    for d in range(1, n_x):
        sends_t.append(
            pltpu.make_async_remote_copy(
                src_ref=total.at[me_x],
                dst_ref=total.at[me_x],
                send_sem=send_t.at[d],
                recv_sem=recv_t.at[d],
                device_id=(lax.rem(me_x + d, n_x), me_y),
                device_id_type=MESH,
            )
        )
        sends_t[-1].start()
    lax.fori_loop(half_levels, levels, advance, 0)
    for store in stores[variables:]:
        store.start()
    for copy in sends_t:
        copy.wait()

    stores.append(pltpu.make_async_copy(total, total_hbm, store_sem.at[2 * variables]))
    stores[-1].start()
    for store in stores:
        store.wait()


def diagonal(block):
    empty = jnp.zeros_like(block)
    return jnp.concatenate(
        [
            jnp.concatenate([block if q == j else empty for j in range(4)], axis=1)
            for q in range(4)
        ],
        axis=0,
    )


def finish(
    partial_hbm, total_hbm, expand_x_hbm, along_y_hbm,
    state_hbm, coeffs_hbm,
    state, total, expand_x, along_y, coeffs, load_sem, store_sem,
):
    count, _, cells_y = state.shape
    n_x, piece = total.shape[:2]
    lines = count // 4 * KW
    loads = [
        pltpu.make_async_copy(total_hbm, total, load_sem.at[0]),
        pltpu.make_async_copy(along_y_hbm.at[lax.axis_index("gy")], along_y, load_sem.at[1]),
        pltpu.make_async_copy(expand_x_hbm.at[lax.axis_index("gx")], expand_x, load_sem.at[2]),
    ]
    for g in range(count // 4):
        block = pl.ds(4 * g, 4)
        loads.append(
            pltpu.make_async_copy(partial_hbm.at[block], state.at[block], load_sem.at[3 + g])
        )
    for load in loads:
        load.start()
    for load in loads[:3]:
        load.wait()
    summed = jnp.concatenate([total[i] for i in range(n_x)], axis=0)[:lines]
    for i in range(count):
        g, q = i // 4, i % 4
        coeffs[i] = summed[g * KW : (g + 1) * KW, q * KW : (q + 1) * KW]
    stores = [pltpu.make_async_copy(coeffs, coeffs_hbm, store_sem.at[0])]
    stores[0].start()
    high, low = split(summed)
    block = diagonal(along_y[0])
    along = dot(jnp.concatenate([high, low], axis=0), block)
    along = along[:lines] + along[lines:] + dot(high, diagonal(along_y[1]))
    for g in range(count // 4):
        high, low = split(along[g * KW : (g + 1) * KW])
        modes = dot(expand_x[...], jnp.concatenate([high, high, low], axis=0))
        loads[3 + g].wait()
        for q in range(4):
            i = 4 * g + q
            state[i] = state[i] - modes[:, q * cells_y : (q + 1) * cells_y]
        block = pl.ds(4 * g, 4)
        stores.append(
            pltpu.make_async_copy(state.at[block], state_hbm.at[block], store_sem.at[g + 1])
        )
        stores[-1].start()
    for store in stores:
        store.wait()


def per_device(sizes, fields, terrain, parent_columns, record_tile, record_cells, record_weights):
    n_x, n_y = sizes
    variables, levels, cells_x, cells_y = fields.shape
    parent_levels, records = parent_columns.shape[1:]
    count = variables * levels
    tile_x, tile_y = cells_x // RATIO, cells_y // RATIO
    row_x = n_x * tile_x
    width = row_x * tile_y
    groups = tile_y // 4
    lines = count // 4 * KW
    piece = -(-lines // (8 * n_x)) * 8
    project_x, expand_x, coarse_x, along_y, coarse_y_table = tables(
        n_x, n_y, cells_x, cells_y, count
    )
    along_y = jnp.asarray(along_y)
    hbm = pl.BlockSpec(memory_space=pltpu.HBM)
    dma = pltpu.SemaphoreType.DMA
    partial_state, summed = pl.pallas_call(
        functools.partial(body, (n_x, n_y, variables, levels, parent_levels)),
        out_shape=(
            jax.ShapeDtypeStruct((count, cells_x, cells_y), F32),
            jax.ShapeDtypeStruct((n_x, piece, 128), F32),
        ),
        in_specs=[hbm] * 10,
        out_specs=(hbm, hbm),
        scratch_shapes=[
            pltpu.VMEM((count, cells_x, cells_y), F32),
            pltpu.VMEM(terrain.shape, jnp.int32),
            pltpu.VMEM(parent_columns.shape, BF16),
            pltpu.VMEM((1, records), jnp.int32),
            pltpu.VMEM((record_cells.shape[1], records), jnp.int32),
            pltpu.VMEM((record_cells.shape[1], records), BF16),
            pltpu.VMEM(coarse_x.shape, BF16),
            pltpu.VMEM((count, cells_x + 16, cells_y), F32),
            pltpu.VMEM((variables * 64, records), F32),
            pltpu.VMEM((variables * 64, width), F32),
            pltpu.VMEM((groups * KW, 4 * row_x), F32),
            pltpu.VMEM((groups, 4 * row_x), F32),
            pltpu.VMEM((n_x, groups, 4 * row_x), F32),
            pltpu.VMEM((2, count, cells_y), F32),
            pltpu.VMEM((2, count, cells_y), F32),
            pltpu.VMEM((2, count, cells_y), F32),
            pltpu.VMEM((2, count, cells_y), F32),
            pltpu.VMEM((2, cells_x, cells_y), F32),
            pltpu.VMEM((n_x, piece, 128), F32),
            pltpu.VMEM((n_x, piece, 128), F32),
            pltpu.VMEM((n_y, piece, 128), F32),
            pltpu.VMEM((n_x, piece, 128), F32),
            pltpu.VMEM(project_x.shape[1:], BF16),
            pltpu.VMEM(along_y.shape[1:], BF16),
            pltpu.VMEM(coarse_y_table.shape[1:], F32),
            pltpu.VMEM((lines, 4 * cells_y), F32),
            dma((11,)), dma((2 * variables + 1,)),
            dma((n_x,)), dma((n_x,)),
            dma((4,)), dma((4,)),
            dma((n_x,)), dma((n_x,)),
            dma((n_y,)), dma((n_y,)),
            dma((n_x,)), dma((n_x,)),
        ],
        compiler_params=pltpu.CompilerParams(
            collective_id=0, has_side_effects=True, vmem_limit_bytes=60 * 1024 * 1024
        ),
        name="nudge",
    )(
        fields.reshape(count, cells_x, cells_y), terrain, parent_columns,
        record_tile.T, record_cells.T, record_weights.T,
        jnp.asarray(project_x), jnp.asarray(coarse_x), along_y, jnp.asarray(coarse_y_table),
    )
    state, coeffs = pl.pallas_call(
        finish,
        out_shape=(
            jax.ShapeDtypeStruct((count, cells_x, cells_y), F32),
            jax.ShapeDtypeStruct((count, KW, KW), F32),
        ),
        in_specs=[hbm] * 4,
        out_specs=(hbm, hbm),
        scratch_shapes=[
            pltpu.VMEM((count, cells_x, cells_y), F32),
            pltpu.VMEM((n_x, piece, 128), F32),
            pltpu.VMEM(expand_x.shape[1:], BF16),
            pltpu.VMEM(along_y.shape[1:], BF16),
            pltpu.VMEM((count, KW, KW), F32),
            dma((count // 4 + 3,)),
            dma((count // 4 + 1,)),
        ],
        compiler_params=pltpu.CompilerParams(vmem_limit_bytes=60 * 1024 * 1024),
        name="finish",
    )(partial_state, summed, jnp.asarray(expand_x), along_y)
    return state.reshape(fields.shape), coeffs.reshape(variables, levels, KW, KW)


def solution(mesh):
    sizes = (mesh.shape["gx"], mesh.shape["gy"])
    return jax.shard_map(
        functools.partial(per_device, sizes),
        mesh=mesh,
        in_specs=(
            P(None, None, "gx", "gy"),
            P("gx", "gy"),
            P(None, None, ("gx", "gy")),
            P(("gx", "gy"), None),
            P(("gx", "gy"), None),
            P(("gx", "gy"), None),
        ),
        out_specs=(P(None, None, "gx", "gy"), P()),
        check_vma=False,
    )
```

```python
import functools
import math

import jax
import jax.numpy as jnp
import ml_dtypes
import numpy as np
from jax import lax
from jax.experimental import pallas as pl
from jax.experimental.pallas import tpu as pltpu
from jax.sharding import PartitionSpec as P

KW = 32
RATIO = 8
TOP = 12000.0
MESH = pl.DeviceIdType.MESH
F32 = jnp.float32
BF16 = jnp.bfloat16
NT = (((1,), (1,)), ((), ()))


def wave_rows(length):
    half = KW // 2
    x = np.arange(length, dtype=np.int64)
    rows = [np.ones(length)]
    for m in range(1, KW):
        if m < half:
            rows.append(math.sqrt(2.0) * np.cos(2.0 * math.pi * ((m * x) % length) / length))
        else:
            rows.append(
                math.sqrt(2.0) * np.sin(2.0 * math.pi * (((m - half + 1) * x) % length) / length)
            )
    return np.stack(rows)


def parts(values):
    values = values.astype(np.float32)
    high = values.astype(ml_dtypes.bfloat16)
    low = (values - high.astype(np.float32)).astype(ml_dtypes.bfloat16)
    return high, low


@functools.lru_cache(maxsize=None)
def tables(n_x, n_y, cells_x, cells_y, fields_count):
    total_x, total_y = n_x * cells_x, n_y * cells_y
    scale = 1.0 / math.sqrt(total_x * total_y)
    basis_x, basis_y = wave_rows(total_x), wave_rows(total_y)
    coarse_y = cells_y // RATIO
    own_x = np.transpose(basis_x.reshape(KW, n_x, cells_x), (1, 0, 2))
    high, low = parts(own_x * scale)
    project_x = np.concatenate(
        [np.concatenate([high, high], 2), np.concatenate([low, np.zeros_like(low)], 2)], 1
    )
    high, low = parts(np.transpose(own_x, (0, 2, 1)) * (4.0 * scale))
    expand_x = np.concatenate([high, low, high], 2)
    at_coarse = basis_x[:, ::RATIO] * (RATIO * RATIO * scale)
    coarse_x = np.kron(np.eye(4), at_coarse)
    coarse_x = np.stack(parts(coarse_x))
    own_y = np.transpose(basis_y.reshape(KW, n_y, cells_y), (1, 0, 2))
    along_y = np.stack(parts(own_y), 1)
    at_rows = np.transpose(basis_y[:, ::RATIO]).reshape(n_y, coarse_y, KW)
    coarse_y_table = np.stack(parts(np.tile(at_rows, (1, 1, fields_count))), 1).astype(np.float32)
    return project_x, expand_x, coarse_x, along_y, coarse_y_table


def split(values):
    high = values.astype(BF16)
    return high, (values - high.astype(F32)).astype(BF16)


def dot(a, b):
    return jnp.dot(a, b, preferred_element_type=F32)


def dot_nt(a, b):
    return lax.dot_general(a, b, NT, preferred_element_type=F32)


def body(
    sizes,
    fields_hbm, terrain_hbm, columns_hbm, tile_hbm, cells_hbm, weights_hbm,
    project_x_hbm, coarse_x_hbm, along_y_hbm, coarse_y_hbm,
    state_hbm, total_hbm,
    state, terrain, columns, tile, cells, weights, coarse_x,
    padded, column_rows, coarse, target, heights, heights_got, edge_rows, edge_rows_got,
    edge_columns, edge_columns_got, turned, partial, partial_got, plane, total,
    project_x, along_y, coarse_y_table, y_terms,
    load_sem, store_sem, send_h, recv_h, send_e, recv_e, send_r, recv_r, send_p, recv_p, send_t, recv_t,
):
    n_x, n_y, variables, levels, parent_levels = sizes
    count = variables * levels
    cells_x, cells_y = terrain.shape
    tile_x, tile_y = cells_x // RATIO, cells_y // RATIO
    row_x = n_x * tile_x
    width = row_x * tile_y
    groups = tile_y // 4
    span = 4 * row_x
    records = tile.shape[1]
    top = 8
    me_x, me_y = lax.axis_index("gx"), lax.axis_index("gy")

    loads = [
        pltpu.make_async_copy(fields_hbm, padded.at[:, pl.ds(top, cells_x), :], load_sem.at[0]),
        pltpu.make_async_copy(project_x_hbm.at[me_x], project_x, load_sem.at[1]),
        pltpu.make_async_copy(along_y_hbm.at[me_y], along_y, load_sem.at[3]),
        pltpu.make_async_copy(coarse_y_hbm.at[me_y], coarse_y_table, load_sem.at[4]),
        pltpu.make_async_copy(coarse_x_hbm, coarse_x, load_sem.at[5]),
    ]
    early = [
        pltpu.make_async_copy(terrain_hbm, terrain, load_sem.at[6]),
        pltpu.make_async_copy(columns_hbm, columns, load_sem.at[7]),
        pltpu.make_async_copy(tile_hbm, tile, load_sem.at[8]),
        pltpu.make_async_copy(cells_hbm, cells, load_sem.at[9]),
        pltpu.make_async_copy(weights_hbm, weights, load_sem.at[10]),
    ]
    for load in early:
        load.start()
    for load in loads:
        load.start()

    edge_rows_got[...] = jnp.zeros_like(edge_rows_got)
    edge_columns_got[...] = jnp.zeros_like(edge_columns_got)
    barrier = pltpu.get_barrier_semaphore()
    for d in range(1, n_x):
        pl.semaphore_signal(
            barrier, inc=1, device_id=(lax.rem(me_x + d, n_x), me_y), device_id_type=MESH
        )
    for d in range(1, n_y):
        pl.semaphore_signal(
            barrier, inc=1, device_id=(me_x, lax.rem(me_y + d, n_y)), device_id_type=MESH
        )

    early[0].wait()
    ground = terrain[pl.ds(0, tile_x, RATIO), :]
    low_bits = ground & 255
    ground = jnp.concatenate(
        [(ground - low_bits).astype(F32), low_bits.astype(F32)], axis=0
    ).astype(BF16)
    for g in range(groups):
        lane = lax.broadcasted_iota(jnp.int32, (1, span), 1)
        row = lax.broadcasted_iota(jnp.int32, (cells_y, span), 0)
        pick = jnp.where(row == RATIO * (4 * g + lane // row_x), 1.0, 0.0).astype(BF16)
        both = dot(ground, pick)
        here = both[:tile_x] + both[tile_x:]
        row = lax.broadcasted_iota(jnp.int32, (tile_x, span), 0)
        here = jnp.where(lane % row_x - me_x * tile_x == row, here, 0.0)
        heights[g : g + 1, :] = jnp.sum(here, axis=0, keepdims=True)

    pl.semaphore_wait(barrier, n_x + n_y - 2)
    sends_h = []
    for d in range(1, n_x):
        sends_h.append(
            pltpu.make_async_remote_copy(
                src_ref=heights,
                dst_ref=heights_got.at[d],
                send_sem=send_h.at[d],
                recv_sem=recv_h.at[d],
                device_id=(lax.rem(me_x + d, n_x), me_y),
                device_id_type=MESH,
            )
        )
        sends_h[-1].start()

    for load in early[1:]:
        load.wait()
    column_rows[...] = jnp.zeros_like(column_rows)
    for v in range(variables):
        column_rows[v * 64 : v * 64 + parent_levels, :] = columns[v].astype(F32)
    packed = column_rows[...].astype(BF16)
    place = cells[...]
    place = (place % tile_y) * row_x + tile[...] * tile_x + place // tile_y
    amount = weights[...].astype(F32)
    entries = place.shape[0]
    merged = []
    for e in range(entries):
        sum_e = jnp.zeros((1, records), F32)
        for f in range(entries):
            sum_e = sum_e + jnp.where(place[f : f + 1] == place[e : e + 1], amount[f : f + 1], 0.0)
        merged.append(sum_e)
    step = 256 if width % 256 == 0 else 128
    line = lax.broadcasted_iota(jnp.int32, (32, records), 0)

    def spread(i, carry):
        highs, lows = [], []
        for part in range(step // 32):
            here = place - (i * step + part * 32)
            matrix = jnp.zeros((32, records), F32)
            for e in range(entries):
                matrix = jnp.where(here[e : e + 1] == line, merged[e], matrix)
            high, low = split(matrix)
            highs.append(high)
            lows.append(low)
        at = pl.ds(pl.multiple_of(i * step, step), step)
        coarse[:, at] = dot_nt(packed, jnp.concatenate(highs, axis=0)) + dot_nt(
            packed, jnp.concatenate(lows, axis=0)
        )
        return carry

    lax.fori_loop(0, width // step, spread, 0)

    for load in loads:
        load.wait()

    block_y = [diagonal(along_y[part]) for part in range(2)]
    for g in range(count // 4):
        highs, lows = [], []
        for i in range(4 * g, 4 * g + 4):
            high, low = split(padded[i, top : top + cells_x, :])
            highs.append(high)
            lows.append(low)
        stacked = jnp.concatenate(
            [jnp.concatenate(highs, axis=1), jnp.concatenate(lows, axis=1)], axis=0
        )
        both = dot(project_x[...], stacked)
        y_terms[g * KW : (g + 1) * KW, :] = both[:KW] + both[KW:]
    high, low = split(y_terms[...])
    nest = dot_nt(jnp.concatenate([high, low], axis=0), block_y[0])
    nest = nest[: high.shape[0]] + nest[high.shape[0] :] + dot_nt(high, block_y[1])

    lane = lax.broadcasted_iota(jnp.int32, (KW, count * KW), 1)
    row = lax.broadcasted_iota(jnp.int32, (KW, count * KW), 0)
    own = lane // KW == row
    spread_y = []
    for part in range(2):
        blocks = []
        for r in range(4):
            for g in range(groups):
                values = coarse_y_table[part, 4 * g + r : 4 * g + r + 1, :]
                blocks.append(jnp.where(own, values, 0.0).astype(BF16))
        spread_y.append(jnp.concatenate(blocks, axis=0))

    for copy in sends_h:
        copy.wait()
    height = heights[...]
    for d in range(1, n_x):
        height = height + heights_got[d]
    heights[...] = height

    level = lax.broadcasted_iota(jnp.int32, (64, 128), 0)
    parent_height = jnp.where(
        level < parent_levels, (level.astype(F32) + 0.5) * (TOP / parent_levels), 1e9
    )
    chunks = span // 128
    for g in range(groups):

        def interpolate(j, carry):
            lanes = pl.ds(pl.multiple_of(j * 128, 128), 128)
            at = pl.ds(pl.multiple_of(g * span + j * 128, 128), 128)
            h = heights[g : g + 1, lanes]
            spacing = (TOP - h) / levels
            inverse = 1.0 / spacing
            base = h * inverse
            scaled = parent_height * inverse
            rows = [[] for _ in range(variables)]
            for k in range(levels):
                hat = jnp.maximum(0.0, 1.0 - jnp.abs((base + (k + 0.5)) - scaled))
                norm = 1.0 / jnp.sum(hat, axis=0, keepdims=True)
                for v in range(variables):
                    value = coarse[v * 64 : (v + 1) * 64, at]
                    rows[v].append(jnp.sum(hat * value, axis=0, keepdims=True) * norm)
            for v in range(variables):
                target[g * KW + v * levels : g * KW + (v + 1) * levels, lanes] = jnp.concatenate(
                    rows[v], axis=0
                )
            target[g * KW + count : (g + 1) * KW, lanes] = jnp.zeros((KW - count, 128), F32)
            return carry

        lax.fori_loop(0, chunks, interpolate, 0)

    high, low = split(target[...])
    along_x = dot_nt(coarse_x[0], high) + dot_nt(coarse_x[0], low) + dot_nt(coarse_x[1], high)
    along_x = jnp.concatenate([along_x[r * KW : (r + 1) * KW] for r in range(4)], axis=1)
    high, low = split(along_x)
    wanted = dot(jnp.concatenate([high, low], axis=0), spread_y[0])
    wanted = wanted[:KW] + wanted[KW:] + dot(high, spread_y[1])

    lines = count // 4 * KW
    difference = [
        nest[g * KW : (g + 1) * KW] - wanted[:, g * 128 : (g + 1) * 128]
        for g in range(count // 4)
    ]
    difference = jnp.concatenate(difference, axis=0)
    piece = partial.shape[1]
    if n_x * piece != lines:
        difference = jnp.concatenate(
            [difference, jnp.zeros((n_x * piece - lines, 128), F32)], axis=0
        )
    for i in range(n_x):
        partial[i] = difference[i * piece : (i + 1) * piece]
    cuts = [0, piece // 16 * 8, piece] if piece > 8 else [0, piece]
    slabs = [pl.ds(a, b - a) for a, b in zip(cuts[:-1], cuts[1:])]
    sends_r = []
    for part, slab in enumerate(slabs):
        sends_r.append([])
        for d in range(1, n_x):
            to = lax.rem(me_x + d, n_x)
            sends_r[part].append(
                pltpu.make_async_remote_copy(
                    src_ref=partial.at[to, slab],
                    dst_ref=partial_got.at[d, slab],
                    send_sem=send_r.at[part, d],
                    recv_sem=recv_r.at[part, d],
                    device_id=(to, me_y),
                    device_id_type=MESH,
                )
            )
            sends_r[part][-1].start()

    edge_rows[0] = padded[:, top, :]
    edge_rows[1] = padded[:, top + cells_x - 1, :]
    lane = lax.broadcasted_iota(jnp.int32, (cells_x, cells_y), 1)
    first = jnp.zeros((cells_x, cells_y), F32)
    last = jnp.zeros((cells_x, cells_y), F32)
    for i in range(count):
        q = padded[i, top : top + cells_x, :]
        first = jnp.where(lane == i, q if i == 0 else pltpu.roll(q, i, 1), first)
        last = jnp.where(lane == i, pltpu.roll(q, i + 1, 1), last)
    for side, columns_here in enumerate((first, last)):
        columns_here = jnp.concatenate(
            [columns_here, jnp.zeros((cells_y - cells_x, cells_y), F32)], axis=0
        )
        edge_columns[side] = jnp.transpose(columns_here)[:count]

    def edge_copy(source, got, side, slot, device):
        return pltpu.make_async_remote_copy(
            src_ref=source.at[side],
            dst_ref=got.at[side],
            send_sem=send_e.at[slot],
            recv_sem=recv_e.at[slot],
            device_id=device,
            device_id_type=MESH,
        )

    down_x = edge_copy(edge_rows, edge_rows_got, 0, 0, (jnp.maximum(me_x - 1, 0), me_y))
    up_x = edge_copy(edge_rows, edge_rows_got, 1, 1, (jnp.minimum(me_x + 1, n_x - 1), me_y))
    down_y = edge_copy(edge_columns, edge_columns_got, 0, 2, (me_x, jnp.maximum(me_y - 1, 0)))
    up_y = edge_copy(edge_columns, edge_columns_got, 1, 3, (me_x, jnp.minimum(me_y + 1, n_y - 1)))
    has_down_x, has_up_x = me_x > 0, me_x < n_x - 1
    has_down_y, has_up_y = me_y > 0, me_y < n_y - 1
    edges = [
        (down_x, has_down_x, has_up_x),
        (up_x, has_up_x, has_down_x),
        (down_y, has_down_y, has_up_y),
        (up_y, has_up_y, has_down_y),
    ]
    for copy, out, _ in edges:
        pl.when(out)(copy.start)

    rows = 32

    def advance(k, carry):
        above_k = jnp.minimum(k + 1, levels - 1)
        below_k = jnp.maximum(k - 1, 0)
        lane = lax.broadcasted_iota(jnp.int32, (rows, cells_y), 1)
        for r in range(0, cells_x, rows):
            here = slice(top + r, top + r + rows)
            metric = TOP / (TOP - terrain[r : r + rows].astype(F32))
            metric = 0.1 * (metric * metric)
            wind_x = 0.05 * padded[k, here, :]
            wind_y = 0.05 * padded[levels + k, here, :]
            for v in range(variables):
                i = v * levels + k
                q = padded[i, here, :]
                east = padded[i, top + r + 1 : top + r + 1 + rows, :]
                west = padded[i, top + r - 1 : top + r - 1 + rows, :]
                north = jnp.where(
                    lane == cells_y - 1,
                    pltpu.roll(turned[0, r : r + rows], cells_y - 1 - i, 1),
                    pltpu.roll(q, cells_y - 1, 1),
                )
                south = jnp.where(
                    lane == 0,
                    pltpu.roll(turned[1, r : r + rows], lax.rem(cells_y - i, cells_y), 1),
                    pltpu.roll(q, 1, 1),
                )
                above = padded[v * levels + above_k, here, :]
                below = padded[v * levels + below_k, here, :]
                transport = wind_x * (east - west) + wind_y * (north - south)
                diffusion = 0.1 * ((east + west) + (north + south) - 4.0 * q)
                mixing = metric * ((above + below) - 2.0 * q)
                state[i, r : r + rows] = q - transport + diffusion + mixing
        return carry

    half_levels = levels // 2
    sends_p = []
    for part, slab in enumerate(slabs):
        for copy in sends_r[part]:
            copy.wait()
        mine = partial[me_x, slab]
        for d in range(1, n_x):
            mine = mine + partial_got[d, slab]
        plane[me_y, slab] = mine
        sends_p.append([])
        for d in range(1, n_y):
            sends_p[part].append(
                pltpu.make_async_remote_copy(
                    src_ref=plane.at[me_y, slab],
                    dst_ref=plane.at[me_y, slab],
                    send_sem=send_p.at[part, d],
                    recv_sem=recv_p.at[part, d],
                    device_id=(me_x, lax.rem(me_y + d, n_y)),
                    device_id_type=MESH,
                )
            )
            sends_p[part][-1].start()
    for copy, out, arrives in edges:
        pl.when(out)(copy.wait_send)
        pl.when(arrives)(copy.wait_recv)
    for side in range(2):
        columns_here = jnp.concatenate(
            [edge_columns_got[side], jnp.zeros((cells_y - count, cells_y), F32)], axis=0
        )
        turned[side] = jnp.transpose(columns_here)[:cells_x]
    padded[:, top + cells_x, :] = edge_rows_got[0]
    padded[:, top - 1, :] = edge_rows_got[1]

    lax.fori_loop(0, half_levels, advance, 0)
    stores = []
    for half in range(2):
        for v in range(variables):
            block = pl.ds(v * levels + half * half_levels, half_levels)
            stores.append(
                pltpu.make_async_copy(
                    state.at[block], state_hbm.at[block], store_sem.at[half * variables + v]
                )
            )
    for store in stores[:variables]:
        store.start()
    sends_t = []
    for part, slab in enumerate(slabs):
        for copy in sends_p[part]:
            copy.wait()
        mine = plane[0, slab]
        for j in range(1, n_y):
            mine = mine + plane[j, slab]
        total[me_x, slab] = mine
        for d in range(1, n_x):
            sends_t.append(
                pltpu.make_async_remote_copy(
                    src_ref=total.at[me_x, slab],
                    dst_ref=total.at[me_x, slab],
                    send_sem=send_t.at[part, d],
                    recv_sem=recv_t.at[part, d],
                    device_id=(lax.rem(me_x + d, n_x), me_y),
                    device_id_type=MESH,
                )
            )
            sends_t[-1].start()
    lax.fori_loop(half_levels, levels, advance, 0)
    for store in stores[variables:]:
        store.start()
    for copy in sends_t:
        copy.wait()

    stores.append(pltpu.make_async_copy(total, total_hbm, store_sem.at[2 * variables]))
    stores[-1].start()
    for store in stores:
        store.wait()


def diagonal(block):
    empty = jnp.zeros_like(block)
    return jnp.concatenate(
        [
            jnp.concatenate([block if q == j else empty for j in range(4)], axis=1)
            for q in range(4)
        ],
        axis=0,
    )


def finish(
    partial_hbm, total_hbm, expand_x_hbm, along_y_hbm,
    state_hbm, coeffs_hbm,
    state, total, expand_x, along_y, coeffs, load_sem, store_sem,
):
    count, _, cells_y = state.shape
    n_x, piece = total.shape[:2]
    lines = count // 4 * KW
    loads = [
        pltpu.make_async_copy(total_hbm, total, load_sem.at[0]),
        pltpu.make_async_copy(along_y_hbm.at[lax.axis_index("gy")], along_y, load_sem.at[1]),
        pltpu.make_async_copy(expand_x_hbm.at[lax.axis_index("gx")], expand_x, load_sem.at[2]),
    ]
    for g in range(count // 4):
        block = pl.ds(4 * g, 4)
        loads.append(
            pltpu.make_async_copy(partial_hbm.at[block], state.at[block], load_sem.at[3 + g])
        )
    for load in loads:
        load.start()
    for load in loads[:3]:
        load.wait()
    summed = jnp.concatenate([total[i] for i in range(n_x)], axis=0)[:lines]
    for i in range(count):
        g, q = i // 4, i % 4
        coeffs[i] = summed[g * KW : (g + 1) * KW, q * KW : (q + 1) * KW]
    stores = [pltpu.make_async_copy(coeffs, coeffs_hbm, store_sem.at[0])]
    stores[0].start()
    high, low = split(summed)
    block = diagonal(along_y[0])
    along = dot(jnp.concatenate([high, low], axis=0), block)
    along = along[:lines] + along[lines:] + dot(high, diagonal(along_y[1]))
    for g in range(count // 4):
        high, low = split(along[g * KW : (g + 1) * KW])
        modes = dot(expand_x[...], jnp.concatenate([high, high, low], axis=0))
        loads[3 + g].wait()
        for q in range(4):
            i = 4 * g + q
            state[i] = state[i] - modes[:, q * cells_y : (q + 1) * cells_y]
        block = pl.ds(4 * g, 4)
        stores.append(
            pltpu.make_async_copy(state.at[block], state_hbm.at[block], store_sem.at[g + 1])
        )
        stores[-1].start()
    for store in stores:
        store.wait()


def per_device(sizes, fields, terrain, parent_columns, record_tile, record_cells, record_weights):
    n_x, n_y = sizes
    variables, levels, cells_x, cells_y = fields.shape
    parent_levels, records = parent_columns.shape[1:]
    count = variables * levels
    tile_x, tile_y = cells_x // RATIO, cells_y // RATIO
    row_x = n_x * tile_x
    width = row_x * tile_y
    groups = tile_y // 4
    lines = count // 4 * KW
    piece = -(-lines // (8 * n_x)) * 8
    project_x, expand_x, coarse_x, along_y, coarse_y_table = tables(
        n_x, n_y, cells_x, cells_y, count
    )
    along_y = jnp.asarray(along_y)
    hbm = pl.BlockSpec(memory_space=pltpu.HBM)
    dma = pltpu.SemaphoreType.DMA
    partial_state, summed = pl.pallas_call(
        functools.partial(body, (n_x, n_y, variables, levels, parent_levels)),
        out_shape=(
            jax.ShapeDtypeStruct((count, cells_x, cells_y), F32),
            jax.ShapeDtypeStruct((n_x, piece, 128), F32),
        ),
        in_specs=[hbm] * 10,
        out_specs=(hbm, hbm),
        scratch_shapes=[
            pltpu.VMEM((count, cells_x, cells_y), F32),
            pltpu.VMEM(terrain.shape, jnp.int32),
            pltpu.VMEM(parent_columns.shape, BF16),
            pltpu.VMEM((1, records), jnp.int32),
            pltpu.VMEM((record_cells.shape[1], records), jnp.int32),
            pltpu.VMEM((record_cells.shape[1], records), BF16),
            pltpu.VMEM(coarse_x.shape, BF16),
            pltpu.VMEM((count, cells_x + 16, cells_y), F32),
            pltpu.VMEM((variables * 64, records), F32),
            pltpu.VMEM((variables * 64, width), F32),
            pltpu.VMEM((groups * KW, 4 * row_x), F32),
            pltpu.VMEM((groups, 4 * row_x), F32),
            pltpu.VMEM((n_x, groups, 4 * row_x), F32),
            pltpu.VMEM((2, count, cells_y), F32),
            pltpu.VMEM((2, count, cells_y), F32),
            pltpu.VMEM((2, count, cells_y), F32),
            pltpu.VMEM((2, count, cells_y), F32),
            pltpu.VMEM((2, cells_x, cells_y), F32),
            pltpu.VMEM((n_x, piece, 128), F32),
            pltpu.VMEM((n_x, piece, 128), F32),
            pltpu.VMEM((n_y, piece, 128), F32),
            pltpu.VMEM((n_x, piece, 128), F32),
            pltpu.VMEM(project_x.shape[1:], BF16),
            pltpu.VMEM(along_y.shape[1:], BF16),
            pltpu.VMEM(coarse_y_table.shape[1:], F32),
            pltpu.VMEM((lines, 4 * cells_y), F32),
            dma((11,)), dma((2 * variables + 1,)),
            dma((n_x,)), dma((n_x,)),
            dma((4,)), dma((4,)),
            dma((2, n_x)), dma((2, n_x)),
            dma((2, n_y)), dma((2, n_y)),
            dma((2, n_x)), dma((2, n_x)),
        ],
        compiler_params=pltpu.CompilerParams(
            collective_id=0, has_side_effects=True, vmem_limit_bytes=60 * 1024 * 1024
        ),
        name="nudge",
    )(
        fields.reshape(count, cells_x, cells_y), terrain, parent_columns,
        record_tile.T, record_cells.T, record_weights.T,
        jnp.asarray(project_x), jnp.asarray(coarse_x), along_y, jnp.asarray(coarse_y_table),
    )
    state, coeffs = pl.pallas_call(
        finish,
        out_shape=(
            jax.ShapeDtypeStruct((count, cells_x, cells_y), F32),
            jax.ShapeDtypeStruct((count, KW, KW), F32),
        ),
        in_specs=[hbm] * 4,
        out_specs=(hbm, hbm),
        scratch_shapes=[
            pltpu.VMEM((count, cells_x, cells_y), F32),
            pltpu.VMEM((n_x, piece, 128), F32),
            pltpu.VMEM(expand_x.shape[1:], BF16),
            pltpu.VMEM(along_y.shape[1:], BF16),
            pltpu.VMEM((count, KW, KW), F32),
            dma((count // 4 + 3,)),
            dma((count // 4 + 1,)),
        ],
        compiler_params=pltpu.CompilerParams(vmem_limit_bytes=60 * 1024 * 1024),
        name="finish",
    )(partial_state, summed, jnp.asarray(expand_x), along_y)
    return state.reshape(fields.shape), coeffs.reshape(variables, levels, KW, KW)


def solution(mesh):
    sizes = (mesh.shape["gx"], mesh.shape["gy"])
    return jax.shard_map(
        functools.partial(per_device, sizes),
        mesh=mesh,
        in_specs=(
            P(None, None, "gx", "gy"),
            P("gx", "gy"),
            P(None, None, ("gx", "gy")),
            P(("gx", "gy"), None),
            P(("gx", "gy"), None),
            P(("gx", "gy"), None),
        ),
        out_specs=(P(None, None, "gx", "gy"), P()),
        check_vma=False,
    )
```

```python
import functools
import math

import jax
import jax.numpy as jnp
import ml_dtypes
import numpy as np
from jax import lax
from jax.experimental import pallas as pl
from jax.experimental.pallas import tpu as pltpu
from jax.sharding import PartitionSpec as P

KW = 32
RATIO = 8
TOP = 12000.0
MESH = pl.DeviceIdType.MESH
F32 = jnp.float32
BF16 = jnp.bfloat16
NT = (((1,), (1,)), ((), ()))


def wave_rows(length):
    half = KW // 2
    x = np.arange(length, dtype=np.int64)
    rows = [np.ones(length)]
    for m in range(1, KW):
        if m < half:
            rows.append(math.sqrt(2.0) * np.cos(2.0 * math.pi * ((m * x) % length) / length))
        else:
            rows.append(
                math.sqrt(2.0) * np.sin(2.0 * math.pi * (((m - half + 1) * x) % length) / length)
            )
    return np.stack(rows)


def parts(values):
    values = values.astype(np.float32)
    high = values.astype(ml_dtypes.bfloat16)
    low = (values - high.astype(np.float32)).astype(ml_dtypes.bfloat16)
    return high, low


@functools.lru_cache(maxsize=None)
def tables(n_x, n_y, cells_x, cells_y, fields_count):
    total_x, total_y = n_x * cells_x, n_y * cells_y
    scale = 1.0 / math.sqrt(total_x * total_y)
    basis_x, basis_y = wave_rows(total_x), wave_rows(total_y)
    coarse_y = cells_y // RATIO
    own_x = np.transpose(basis_x.reshape(KW, n_x, cells_x), (1, 0, 2))
    high, low = parts(own_x * scale)
    project_x = np.concatenate(
        [np.concatenate([high, high], 2), np.concatenate([low, np.zeros_like(low)], 2)], 1
    )
    high, low = parts(np.transpose(own_x, (0, 2, 1)) * (4.0 * scale))
    expand_x = np.concatenate([high, low, high], 2)
    at_coarse = basis_x[:, ::RATIO] * (RATIO * RATIO * scale)
    coarse_x = np.kron(np.eye(4), at_coarse)
    coarse_x = np.stack(parts(coarse_x))
    own_y = np.transpose(basis_y.reshape(KW, n_y, cells_y), (1, 0, 2))
    along_y = np.stack(parts(own_y), 1)
    at_rows = np.transpose(basis_y[:, ::RATIO]).reshape(n_y, coarse_y, KW)
    coarse_y_table = np.stack(parts(np.tile(at_rows, (1, 1, fields_count))), 1).astype(np.float32)
    return project_x, expand_x, coarse_x, along_y, coarse_y_table


def split(values):
    high = values.astype(BF16)
    return high, (values - high.astype(F32)).astype(BF16)


def dot(a, b):
    return jnp.dot(a, b, preferred_element_type=F32)


def dot_nt(a, b):
    return lax.dot_general(a, b, NT, preferred_element_type=F32)


def body(
    sizes,
    fields_hbm, terrain_hbm, columns, tile_hbm, cells_hbm, weights,
    project_x_hbm, coarse_x_hbm, along_y_hbm, coarse_y_hbm,
    state_hbm, total_hbm,
    state, terrain, tile, cells, coarse_x,
    padded, column_rows, coarse, target, heights, heights_got, edge_rows, edge_rows_got,
    edge_columns, edge_columns_got, turned, partial, partial_got, plane, total,
    project_x, along_y, coarse_y_table, y_terms,
    load_sem, store_sem, send_h, recv_h, send_e, recv_e, send_r, recv_r, send_p, recv_p, send_t, recv_t,
):
    n_x, n_y, variables, levels, parent_levels = sizes
    count = variables * levels
    cells_x, cells_y = terrain.shape
    tile_x, tile_y = cells_x // RATIO, cells_y // RATIO
    row_x = n_x * tile_x
    width = row_x * tile_y
    groups = tile_y // 4
    span = 4 * row_x
    records = tile.shape[1]
    top = 8
    me_x, me_y = lax.axis_index("gx"), lax.axis_index("gy")

    loads = [
        pltpu.make_async_copy(fields_hbm, padded.at[:, pl.ds(top, cells_x), :], load_sem.at[0]),
        pltpu.make_async_copy(project_x_hbm.at[me_x], project_x, load_sem.at[1]),
        pltpu.make_async_copy(along_y_hbm.at[me_y], along_y, load_sem.at[3]),
        pltpu.make_async_copy(coarse_y_hbm.at[me_y], coarse_y_table, load_sem.at[4]),
        pltpu.make_async_copy(coarse_x_hbm, coarse_x, load_sem.at[5]),
    ]
    early = [
        pltpu.make_async_copy(terrain_hbm, terrain, load_sem.at[6]),
        pltpu.make_async_copy(tile_hbm, tile, load_sem.at[8]),
        pltpu.make_async_copy(cells_hbm, cells, load_sem.at[9]),
    ]
    for load in early:
        load.start()
    for load in loads:
        load.start()

    edge_rows_got[...] = jnp.zeros_like(edge_rows_got)
    edge_columns_got[...] = jnp.zeros_like(edge_columns_got)
    barrier = pltpu.get_barrier_semaphore()
    for d in range(1, n_x):
        pl.semaphore_signal(
            barrier, inc=1, device_id=(lax.rem(me_x + d, n_x), me_y), device_id_type=MESH
        )
    for d in range(1, n_y):
        pl.semaphore_signal(
            barrier, inc=1, device_id=(me_x, lax.rem(me_y + d, n_y)), device_id_type=MESH
        )

    early[0].wait()
    ground = terrain[pl.ds(0, tile_x, RATIO), :]
    low_bits = ground & 255
    ground = jnp.concatenate(
        [(ground - low_bits).astype(F32), low_bits.astype(F32)], axis=0
    ).astype(BF16)
    for g in range(groups):
        lane = lax.broadcasted_iota(jnp.int32, (1, span), 1)
        row = lax.broadcasted_iota(jnp.int32, (cells_y, span), 0)
        pick = jnp.where(row == RATIO * (4 * g + lane // row_x), 1.0, 0.0).astype(BF16)
        both = dot(ground, pick)
        here = both[:tile_x] + both[tile_x:]
        row = lax.broadcasted_iota(jnp.int32, (tile_x, span), 0)
        here = jnp.where(lane % row_x - me_x * tile_x == row, here, 0.0)
        heights[g : g + 1, :] = jnp.sum(here, axis=0, keepdims=True)

    pl.semaphore_wait(barrier, n_x + n_y - 2)
    sends_h = []
    for d in range(1, n_x):
        sends_h.append(
            pltpu.make_async_remote_copy(
                src_ref=heights,
                dst_ref=heights_got.at[d],
                send_sem=send_h.at[d],
                recv_sem=recv_h.at[d],
                device_id=(lax.rem(me_x + d, n_x), me_y),
                device_id_type=MESH,
            )
        )
        sends_h[-1].start()

    for load in early[1:]:
        load.wait()
    column_rows[...] = jnp.zeros_like(column_rows)
    for v in range(variables):
        column_rows[v * 64 : v * 64 + parent_levels, :] = columns[v].astype(F32)
    packed = column_rows[...].astype(BF16)
    place = cells[...]
    place = (place % tile_y) * row_x + tile[...] * tile_x + place // tile_y
    amount = weights[...].astype(F32)
    entries = place.shape[0]
    merged = []
    for e in range(entries):
        sum_e = jnp.zeros((1, records), F32)
        for f in range(entries):
            sum_e = sum_e + jnp.where(place[f : f + 1] == place[e : e + 1], amount[f : f + 1], 0.0)
        merged.append(sum_e)
    step = 256 if width % 256 == 0 else 128
    line = lax.broadcasted_iota(jnp.int32, (32, records), 0)

    def spread(i, carry):
        highs, lows = [], []
        for part in range(step // 32):
            here = place - (i * step + part * 32)
            matrix = jnp.zeros((32, records), F32)
            for e in range(entries):
                matrix = jnp.where(here[e : e + 1] == line, merged[e], matrix)
            high, low = split(matrix)
            highs.append(high)
            lows.append(low)
        at = pl.ds(pl.multiple_of(i * step, step), step)
        coarse[:, at] = dot_nt(packed, jnp.concatenate(highs, axis=0)) + dot_nt(
            packed, jnp.concatenate(lows, axis=0)
        )
        return carry

    lax.fori_loop(0, width // step, spread, 0)

    for load in loads:
        load.wait()

    block_y = [diagonal(along_y[part]) for part in range(2)]
    for g in range(count // 4):
        highs, lows = [], []
        for i in range(4 * g, 4 * g + 4):
            high, low = split(padded[i, top : top + cells_x, :])
            highs.append(high)
            lows.append(low)
        stacked = jnp.concatenate(
            [jnp.concatenate(highs, axis=1), jnp.concatenate(lows, axis=1)], axis=0
        )
        both = dot(project_x[...], stacked)
        y_terms[g * KW : (g + 1) * KW, :] = both[:KW] + both[KW:]
    high, low = split(y_terms[...])
    nest = dot_nt(jnp.concatenate([high, low], axis=0), block_y[0])
    nest = nest[: high.shape[0]] + nest[high.shape[0] :] + dot_nt(high, block_y[1])

    lane = lax.broadcasted_iota(jnp.int32, (KW, count * KW), 1)
    row = lax.broadcasted_iota(jnp.int32, (KW, count * KW), 0)
    own = lane // KW == row
    spread_y = []
    for part in range(2):
        blocks = []
        for r in range(4):
            for g in range(groups):
                values = coarse_y_table[part, 4 * g + r : 4 * g + r + 1, :]
                blocks.append(jnp.where(own, values, 0.0).astype(BF16))
        spread_y.append(jnp.concatenate(blocks, axis=0))

    for copy in sends_h:
        copy.wait()
    height = heights[...]
    for d in range(1, n_x):
        height = height + heights_got[d]
    heights[...] = height

    level = lax.broadcasted_iota(jnp.int32, (64, 128), 0)
    parent_height = jnp.where(
        level < parent_levels, (level.astype(F32) + 0.5) * (TOP / parent_levels), 1e9
    )
    chunks = span // 128
    for g in range(groups):

        def interpolate(j, carry):
            lanes = pl.ds(pl.multiple_of(j * 128, 128), 128)
            at = pl.ds(pl.multiple_of(g * span + j * 128, 128), 128)
            h = heights[g : g + 1, lanes]
            spacing = (TOP - h) / levels
            inverse = 1.0 / spacing
            base = h * inverse
            scaled = parent_height * inverse
            rows = [[] for _ in range(variables)]
            for k in range(levels):
                hat = jnp.maximum(0.0, 1.0 - jnp.abs((base + (k + 0.5)) - scaled))
                norm = 1.0 / jnp.sum(hat, axis=0, keepdims=True)
                for v in range(variables):
                    value = coarse[v * 64 : (v + 1) * 64, at]
                    rows[v].append(jnp.sum(hat * value, axis=0, keepdims=True) * norm)
            for v in range(variables):
                target[g * KW + v * levels : g * KW + (v + 1) * levels, lanes] = jnp.concatenate(
                    rows[v], axis=0
                )
            target[g * KW + count : (g + 1) * KW, lanes] = jnp.zeros((KW - count, 128), F32)
            return carry

        lax.fori_loop(0, chunks, interpolate, 0)

    high, low = split(target[...])
    along_x = dot_nt(coarse_x[0], high) + dot_nt(coarse_x[0], low) + dot_nt(coarse_x[1], high)
    along_x = jnp.concatenate([along_x[r * KW : (r + 1) * KW] for r in range(4)], axis=1)
    high, low = split(along_x)
    wanted = dot(jnp.concatenate([high, low], axis=0), spread_y[0])
    wanted = wanted[:KW] + wanted[KW:] + dot(high, spread_y[1])

    lines = count // 4 * KW
    difference = [
        nest[g * KW : (g + 1) * KW] - wanted[:, g * 128 : (g + 1) * 128]
        for g in range(count // 4)
    ]
    difference = jnp.concatenate(difference, axis=0)
    piece = partial.shape[1]
    if n_x * piece != lines:
        difference = jnp.concatenate(
            [difference, jnp.zeros((n_x * piece - lines, 128), F32)], axis=0
        )
    for i in range(n_x):
        partial[i] = difference[i * piece : (i + 1) * piece]
    sends_r = []
    for d in range(1, n_x):
        to = lax.rem(me_x + d, n_x)
        sends_r.append(
            pltpu.make_async_remote_copy(
                src_ref=partial.at[to],
                dst_ref=partial_got.at[d],
                send_sem=send_r.at[d],
                recv_sem=recv_r.at[d],
                device_id=(to, me_y),
                device_id_type=MESH,
            )
        )
        sends_r[-1].start()

    edge_rows[0] = padded[:, top, :]
    edge_rows[1] = padded[:, top + cells_x - 1, :]
    lane = lax.broadcasted_iota(jnp.int32, (cells_x, cells_y), 1)
    first = jnp.zeros((cells_x, cells_y), F32)
    last = jnp.zeros((cells_x, cells_y), F32)
    for i in range(count):
        q = padded[i, top : top + cells_x, :]
        first = jnp.where(lane == i, q if i == 0 else pltpu.roll(q, i, 1), first)
        last = jnp.where(lane == i, pltpu.roll(q, i + 1, 1), last)
    for side, columns_here in enumerate((first, last)):
        columns_here = jnp.concatenate(
            [columns_here, jnp.zeros((cells_y - cells_x, cells_y), F32)], axis=0
        )
        edge_columns[side] = jnp.transpose(columns_here)[:count]

    def edge_copy(source, got, side, slot, device):
        return pltpu.make_async_remote_copy(
            src_ref=source.at[side],
            dst_ref=got.at[side],
            send_sem=send_e.at[slot],
            recv_sem=recv_e.at[slot],
            device_id=device,
            device_id_type=MESH,
        )

    down_x = edge_copy(edge_rows, edge_rows_got, 0, 0, (jnp.maximum(me_x - 1, 0), me_y))
    up_x = edge_copy(edge_rows, edge_rows_got, 1, 1, (jnp.minimum(me_x + 1, n_x - 1), me_y))
    down_y = edge_copy(edge_columns, edge_columns_got, 0, 2, (me_x, jnp.maximum(me_y - 1, 0)))
    up_y = edge_copy(edge_columns, edge_columns_got, 1, 3, (me_x, jnp.minimum(me_y + 1, n_y - 1)))
    has_down_x, has_up_x = me_x > 0, me_x < n_x - 1
    has_down_y, has_up_y = me_y > 0, me_y < n_y - 1
    edges = [
        (down_x, has_down_x, has_up_x),
        (up_x, has_up_x, has_down_x),
        (down_y, has_down_y, has_up_y),
        (up_y, has_up_y, has_down_y),
    ]
    for copy, out, _ in edges:
        pl.when(out)(copy.start)

    rows = 32

    def advance(k, carry):
        above_k = jnp.minimum(k + 1, levels - 1)
        below_k = jnp.maximum(k - 1, 0)
        lane = lax.broadcasted_iota(jnp.int32, (rows, cells_y), 1)
        for r in range(0, cells_x, rows):
            here = slice(top + r, top + r + rows)
            metric = TOP / (TOP - terrain[r : r + rows].astype(F32))
            metric = 0.1 * (metric * metric)
            wind_x = 0.05 * padded[k, here, :]
            wind_y = 0.05 * padded[levels + k, here, :]
            for v in range(variables):
                i = v * levels + k
                q = padded[i, here, :]
                east = padded[i, top + r + 1 : top + r + 1 + rows, :]
                west = padded[i, top + r - 1 : top + r - 1 + rows, :]
                north = jnp.where(
                    lane == cells_y - 1,
                    pltpu.roll(turned[0, r : r + rows], cells_y - 1 - i, 1),
                    pltpu.roll(q, cells_y - 1, 1),
                )
                south = jnp.where(
                    lane == 0,
                    pltpu.roll(turned[1, r : r + rows], lax.rem(cells_y - i, cells_y), 1),
                    pltpu.roll(q, 1, 1),
                )
                above = padded[v * levels + above_k, here, :]
                below = padded[v * levels + below_k, here, :]
                transport = wind_x * (east - west) + wind_y * (north - south)
                diffusion = 0.1 * ((east + west) + (north + south) - 4.0 * q)
                mixing = metric * ((above + below) - 2.0 * q)
                state[i, r : r + rows] = q - transport + diffusion + mixing
        return carry

    half_levels = levels // 2
    for copy in sends_r:
        copy.wait()
    mine = partial[me_x]
    for d in range(1, n_x):
        mine = mine + partial_got[d]
    plane[me_y] = mine
    sends_p = []
    for d in range(1, n_y):
        sends_p.append(
            pltpu.make_async_remote_copy(
                src_ref=plane.at[me_y],
                dst_ref=plane.at[me_y],
                send_sem=send_p.at[d],
                recv_sem=recv_p.at[d],
                device_id=(me_x, lax.rem(me_y + d, n_y)),
                device_id_type=MESH,
            )
        )
        sends_p[-1].start()
    for copy, out, arrives in edges:
        pl.when(out)(copy.wait_send)
        pl.when(arrives)(copy.wait_recv)
    for side in range(2):
        columns_here = jnp.concatenate(
            [edge_columns_got[side], jnp.zeros((cells_y - count, cells_y), F32)], axis=0
        )
        turned[side] = jnp.transpose(columns_here)[:cells_x]
    padded[:, top + cells_x, :] = edge_rows_got[0]
    padded[:, top - 1, :] = edge_rows_got[1]

    lax.fori_loop(0, half_levels, advance, 0)
    stores = []
    for half in range(2):
        for v in range(variables):
            block = pl.ds(v * levels + half * half_levels, half_levels)
            stores.append(
                pltpu.make_async_copy(
                    state.at[block], state_hbm.at[block], store_sem.at[half * variables + v]
                )
            )
    for store in stores[:variables]:
        store.start()
    for copy in sends_p:
        copy.wait()
    mine = plane[0]
    for j in range(1, n_y):
        mine = mine + plane[j]
    total[me_x] = mine
    sends_t = []
    for d in range(1, n_x):
        sends_t.append(
            pltpu.make_async_remote_copy(
                src_ref=total.at[me_x],
                dst_ref=total.at[me_x],
                send_sem=send_t.at[d],
                recv_sem=recv_t.at[d],
                device_id=(lax.rem(me_x + d, n_x), me_y),
                device_id_type=MESH,
            )
        )
        sends_t[-1].start()
    lax.fori_loop(half_levels, levels, advance, 0)
    for store in stores[variables:]:
        store.start()
    for copy in sends_t:
        copy.wait()

    stores.append(pltpu.make_async_copy(total, total_hbm, store_sem.at[2 * variables]))
    stores[-1].start()
    for store in stores:
        store.wait()


def diagonal(block):
    empty = jnp.zeros_like(block)
    return jnp.concatenate(
        [
            jnp.concatenate([block if q == j else empty for j in range(4)], axis=1)
            for q in range(4)
        ],
        axis=0,
    )


def finish(
    partial_hbm, total_hbm, expand_x_hbm, along_y_hbm,
    state_hbm, coeffs_hbm,
    state, total, expand_x, along_y, coeffs, load_sem, store_sem,
):
    count, _, cells_y = state.shape
    n_x, piece = total.shape[:2]
    lines = count // 4 * KW
    loads = [
        pltpu.make_async_copy(total_hbm, total, load_sem.at[0]),
        pltpu.make_async_copy(along_y_hbm.at[lax.axis_index("gy")], along_y, load_sem.at[1]),
        pltpu.make_async_copy(expand_x_hbm.at[lax.axis_index("gx")], expand_x, load_sem.at[2]),
    ]
    for g in range(count // 4):
        block = pl.ds(4 * g, 4)
        loads.append(
            pltpu.make_async_copy(partial_hbm.at[block], state.at[block], load_sem.at[3 + g])
        )
    for load in loads:
        load.start()
    for load in loads[:3]:
        load.wait()
    summed = jnp.concatenate([total[i] for i in range(n_x)], axis=0)[:lines]
    for i in range(count):
        g, q = i // 4, i % 4
        coeffs[i] = summed[g * KW : (g + 1) * KW, q * KW : (q + 1) * KW]
    stores = [pltpu.make_async_copy(coeffs, coeffs_hbm, store_sem.at[0])]
    stores[0].start()
    high, low = split(summed)
    block = diagonal(along_y[0])
    along = dot(jnp.concatenate([high, low], axis=0), block)
    along = along[:lines] + along[lines:] + dot(high, diagonal(along_y[1]))
    for g in range(count // 4):
        high, low = split(along[g * KW : (g + 1) * KW])
        modes = dot(expand_x[...], jnp.concatenate([high, high, low], axis=0))
        loads[3 + g].wait()
        for q in range(4):
            i = 4 * g + q
            state[i] = state[i] - modes[:, q * cells_y : (q + 1) * cells_y]
        block = pl.ds(4 * g, 4)
        stores.append(
            pltpu.make_async_copy(state.at[block], state_hbm.at[block], store_sem.at[g + 1])
        )
        stores[-1].start()
    for store in stores:
        store.wait()


def per_device(sizes, fields, terrain, parent_columns, record_tile, record_cells, record_weights):
    n_x, n_y = sizes
    variables, levels, cells_x, cells_y = fields.shape
    parent_levels, records = parent_columns.shape[1:]
    count = variables * levels
    tile_x, tile_y = cells_x // RATIO, cells_y // RATIO
    row_x = n_x * tile_x
    width = row_x * tile_y
    groups = tile_y // 4
    lines = count // 4 * KW
    piece = -(-lines // (8 * n_x)) * 8
    project_x, expand_x, coarse_x, along_y, coarse_y_table = tables(
        n_x, n_y, cells_x, cells_y, count
    )
    along_y = jnp.asarray(along_y)
    vmem = pl.BlockSpec(memory_space=pltpu.VMEM)
    hbm = pl.BlockSpec(memory_space=pltpu.HBM)
    dma = pltpu.SemaphoreType.DMA
    partial_state, summed = pl.pallas_call(
        functools.partial(body, (n_x, n_y, variables, levels, parent_levels)),
        out_shape=(
            jax.ShapeDtypeStruct((count, cells_x, cells_y), F32),
            jax.ShapeDtypeStruct((n_x, piece, 128), F32),
        ),
        in_specs=[hbm, hbm, vmem, hbm, hbm, vmem] + [hbm] * 4,
        out_specs=(hbm, hbm),
        scratch_shapes=[
            pltpu.VMEM((count, cells_x, cells_y), F32),
            pltpu.VMEM(terrain.shape, jnp.int32),
            pltpu.VMEM((1, records), jnp.int32),
            pltpu.VMEM((record_cells.shape[1], records), jnp.int32),
            pltpu.VMEM(coarse_x.shape, BF16),
            pltpu.VMEM((count, cells_x + 16, cells_y), F32),
            pltpu.VMEM((variables * 64, records), F32),
            pltpu.VMEM((variables * 64, width), F32),
            pltpu.VMEM((groups * KW, 4 * row_x), F32),
            pltpu.VMEM((groups, 4 * row_x), F32),
            pltpu.VMEM((n_x, groups, 4 * row_x), F32),
            pltpu.VMEM((2, count, cells_y), F32),
            pltpu.VMEM((2, count, cells_y), F32),
            pltpu.VMEM((2, count, cells_y), F32),
            pltpu.VMEM((2, count, cells_y), F32),
            pltpu.VMEM((2, cells_x, cells_y), F32),
            pltpu.VMEM((n_x, piece, 128), F32),
            pltpu.VMEM((n_x, piece, 128), F32),
            pltpu.VMEM((n_y, piece, 128), F32),
            pltpu.VMEM((n_x, piece, 128), F32),
            pltpu.VMEM(project_x.shape[1:], BF16),
            pltpu.VMEM(along_y.shape[1:], BF16),
            pltpu.VMEM(coarse_y_table.shape[1:], F32),
            pltpu.VMEM((lines, 4 * cells_y), F32),
            dma((11,)), dma((2 * variables + 1,)),
            dma((n_x,)), dma((n_x,)),
            dma((4,)), dma((4,)),
            dma((n_x,)), dma((n_x,)),
            dma((n_y,)), dma((n_y,)),
            dma((n_x,)), dma((n_x,)),
        ],
        compiler_params=pltpu.CompilerParams(
            collective_id=0, has_side_effects=True, vmem_limit_bytes=60 * 1024 * 1024
        ),
        name="nudge",
    )(
        fields.reshape(count, cells_x, cells_y), terrain, parent_columns,
        record_tile.T, record_cells.T, record_weights.T,
        jnp.asarray(project_x), jnp.asarray(coarse_x), along_y, jnp.asarray(coarse_y_table),
    )
    state, coeffs = pl.pallas_call(
        finish,
        out_shape=(
            jax.ShapeDtypeStruct((count, cells_x, cells_y), F32),
            jax.ShapeDtypeStruct((count, KW, KW), F32),
        ),
        in_specs=[hbm] * 4,
        out_specs=(hbm, hbm),
        scratch_shapes=[
            pltpu.VMEM((count, cells_x, cells_y), F32),
            pltpu.VMEM((n_x, piece, 128), F32),
            pltpu.VMEM(expand_x.shape[1:], BF16),
            pltpu.VMEM(along_y.shape[1:], BF16),
            pltpu.VMEM((count, KW, KW), F32),
            dma((count // 4 + 3,)),
            dma((count // 4 + 1,)),
        ],
        compiler_params=pltpu.CompilerParams(vmem_limit_bytes=60 * 1024 * 1024),
        name="finish",
    )(partial_state, summed, jnp.asarray(expand_x), along_y)
    return state.reshape(fields.shape), coeffs.reshape(variables, levels, KW, KW)


def solution(mesh):
    sizes = (mesh.shape["gx"], mesh.shape["gy"])
    return jax.shard_map(
        functools.partial(per_device, sizes),
        mesh=mesh,
        in_specs=(
            P(None, None, "gx", "gy"),
            P("gx", "gy"),
            P(None, None, ("gx", "gy")),
            P(("gx", "gy"), None),
            P(("gx", "gy"), None),
            P(("gx", "gy"), None),
        ),
        out_specs=(P(None, None, "gx", "gy"), P()),
        check_vma=False,
    )
```
